256 devices in a mesh: dp: 32 (over z, x), mp: 8 (over y, core).
Axes of the slice: x: 4, y: 4, z: 8, core: 2. Of those that a mesh axis runs over, the one named last changes fastest.
Arguments:
- qkv_rows: bfloat16 [16384, 3, 3072], P('dp', None, 'mp'), may hold values from -8 to 8
- out_weight: bfloat16 [3072, 6144], P('mp'), may hold values from -0.109375 to 0.109375
- out_grad: bfloat16 [12288, 6144], P('dp', 'mp'), may hold values from -6 to 6
- image_len: int32 [256], replicated, may hold values from 0 to 256, as said below
- dest_rank: int32 [256], replicated, may hold values from 0 to 31, as said below
- dest_offset: int32 [256], replicated, may hold values from 0 to 320, as said below
Outputs:
- mixed: bfloat16 [12288, 6144], P('dp', 'mp')
- qkv_grad: bfloat16 [16384, 3, 3072], P('dp', None, 'mp')
- weight_grad: bfloat16 [3072, 6144], P('mp', 'dp')
The draws below stay inside these ranges and needn't reach their ends.
Inputs may be any that keep to these rules, and one draw needn't show every extreme that they name: `image_len`: patch counts are multiples of 64; 0 marks an empty slot, whose rank is its own and whose offset is 0. Every rank holds 5, 6, 7 or 8 times 64 rows from row 0 and at least one image has 256 patches. `dest_rank`: only slots 5, 6 and 7 move, each with 64 patches: slot 6 of rank r goes to rank (r + 1) mod 32, slot 7 to rank (r - 1) mod 32, slot 5 to rank (r + 32 / 2) mod 32, all at offset 5 * 64; a rank receives at most one image; an image that stays keeps its rows, which lie below 384; after the moves every rank holds exactly 384 rows. `dest_offset`: multiples of 64; images of one rank after the moves don't share rows.
All inputs are finite; a program needn't handle non-finite values.
Results may differ from the reference program's by a relative error of at most 0.025.
Values may be sent and summed in bfloat16 or wider, within the bound.
A program may use at most 128 MiB of HBM per device.

```python
import jax
import jax.numpy as jnp
from jax import lax

D = 6144
HEAD = 128
UNIT = 64
SLOTS = 8
HOME = 512
CAP = 384
INNER = 3072
WORK_ALL = 12288
N_DP = 32
N_MP = 8


def plan_tables(key):
    rank_ids = jnp.arange(N_DP, dtype=jnp.int32)
    phase = jax.random.randint(jax.random.fold_in(key, 101), (), 0, 4).astype(jnp.int32)
    group = jnp.remainder(rank_ids - phase, 4)
    lower = rank_ids < N_DP // 2
    sends_across = (group == 2) & lower
    fill_units = jnp.where((group == 0) | sends_across, 6, 5)
    part_units = jax.random.randint(jax.random.fold_in(key, 102), (N_DP, 5), 2, 5).astype(jnp.int32)
    big_rank = jax.random.randint(jax.random.fold_in(key, 103), (), 0, N_DP).astype(jnp.int32)
    first_slot = (rank_ids[:, None] == big_rank) & (jnp.arange(5, dtype=jnp.int32)[None, :] == 0)
    part_units = jnp.where(first_slot, 4, part_units)
    before = jnp.cumsum(part_units, axis=1) - part_units
    stay_units = jnp.clip(fill_units[:, None] - before, 0, part_units)
    heavy = (group == 0).astype(jnp.int32)
    moved_units = jnp.stack([sends_across.astype(jnp.int32), heavy, heavy], axis=1)
    unit_table = jnp.concatenate([stay_units, moved_units], axis=1)
    len_table = UNIT * unit_table
    start_table = jnp.cumsum(len_table, axis=1) - len_table
    partner_next = jnp.remainder(rank_ids + 1, N_DP)
    partner_prev = jnp.remainder(rank_ids + N_DP - 1, N_DP)
    partner_across = jnp.remainder(rank_ids + N_DP // 2, N_DP)
    slot_ids = jnp.arange(SLOTS, dtype=jnp.int32)[None, :]
    dest_table = jnp.where(slot_ids == 5, partner_across[:, None], jnp.where(slot_ids == 6, partner_next[:, None], jnp.where(slot_ids == 7, partner_prev[:, None], rank_ids[:, None])))
    dest_table = jnp.where(len_table > 0, dest_table, rank_ids[:, None])
    offset_table = jnp.where(slot_ids >= 5, 5 * UNIT, start_table)
    offset_table = jnp.where(len_table > 0, offset_table, 0)
    return (len_table.reshape(-1), dest_table.reshape(-1), offset_table.reshape(-1))


def draw_image_len(key, part):
    return plan_tables(key)[0].astype(jnp.int32)


def draw_dest_rank(key, part):
    return plan_tables(key)[1].astype(jnp.int32)


def draw_dest_offset(key, part):
    return plan_tables(key)[2].astype(jnp.int32)


def draw_qkv_rows(key, part):
    key = jax.random.fold_in(key, 7)
    total_rows = HOME * N_DP
    base = jnp.clip(jax.random.normal(jax.random.fold_in(key, 1), (total_rows, 3, INNER), jnp.float32), -8.0, 8.0)
    return base.astype(jnp.bfloat16)


def shard_levels(rng, dims, cuts, smallest, largest):
    def one(axis_at, blocks):
        draws = jax.random.uniform(jax.random.fold_in(jax.random.fold_in(rng, 6), axis_at), (blocks,), jnp.float32, smallest / len(cuts), largest / len(cuts))
        return jnp.repeat(jnp.exp(draws), dims[axis_at] // blocks).reshape((-1,) + (1,) * (len(dims) - axis_at - 1))

    gain = one(*cuts[0])
    for cut in cuts[1:]:
        gain = gain * one(*cut)
    return gain


def centred(own_key, shape, width, limit, pieces=(), kind=jnp.bfloat16):
    factor_of = shard_levels(own_key, shape, pieces, -0.22, 0.18) if pieces else 1.0
    values = jax.random.normal(own_key, shape, jnp.float32) * width * factor_of
    return jnp.minimum(jnp.maximum(values, -limit), limit).astype(kind)


def setup_inputs(seed: int = 0) -> dict:
    arg_keys = jax.random.split(jax.random.key(seed), 7)
    qkv_rows = draw_qkv_rows(jax.random.fold_in(arg_keys[6], 71), 0)
    out_weight = centred(arg_keys[1], (INNER, D), INNER ** -0.5, 0.109375, ((0, 8),))
    out_grad = centred(arg_keys[2], (WORK_ALL, D), 1.0, 6.0, ((0, 32), (1, 8)))
    image_len = draw_image_len(jax.random.fold_in(arg_keys[6], 71), 0)
    dest_rank = draw_dest_rank(jax.random.fold_in(arg_keys[6], 71), 0)
    dest_offset = draw_dest_offset(jax.random.fold_in(arg_keys[6], 71), 0)
    return {"qkv_rows": qkv_rows, "out_weight": out_weight, "out_grad": out_grad, "image_len": image_len, "dest_rank": dest_rank, "dest_offset": dest_offset}


def attend(qkv_block, seg_ids):
    row_count = qkv_block.shape[0]
    head_count = qkv_block.shape[2] // HEAD
    queries = qkv_block[:, 0].reshape(row_count, head_count, HEAD).astype(jnp.float32)
    keys_part = qkv_block[:, 1].reshape(row_count, head_count, HEAD).astype(jnp.float32)
    values_part = qkv_block[:, 2].reshape(row_count, head_count, HEAD).astype(jnp.float32)
    scores = jnp.einsum("qhd,khd->hqk", queries, keys_part) * (HEAD ** -0.5)
    allowed = ((seg_ids[:, None] == seg_ids[None, :]) & (seg_ids[:, None] >= 0)) | jnp.eye(row_count, dtype=bool)
    scores = jnp.where(allowed[None], scores, -1e30)
    row_max = jnp.max(scores, axis=-1, keepdims=True)
    weights = jnp.exp(scores - row_max)
    probs = weights / jnp.sum(weights, axis=-1, keepdims=True)
    probs_b = probs.astype(jnp.bfloat16)
    output = jnp.einsum("hqk,khd->qhd", probs_b.astype(jnp.float32), values_part)
    return output.reshape(row_count, head_count * HEAD).astype(jnp.bfloat16), probs, probs_b


def attend_back(qkv_block, seg_ids, grad_block):
    row_count = qkv_block.shape[0]
    head_count = qkv_block.shape[2] // HEAD
    unused, probs, probs_b = attend(qkv_block, seg_ids)
    queries = qkv_block[:, 0].reshape(row_count, head_count, HEAD).astype(jnp.float32)
    keys_part = qkv_block[:, 1].reshape(row_count, head_count, HEAD).astype(jnp.float32)
    values_part = qkv_block[:, 2].reshape(row_count, head_count, HEAD).astype(jnp.float32)
    grads = grad_block.reshape(row_count, head_count, HEAD).astype(jnp.float32)
    dprob = jnp.einsum("qhd,khd->hqk", grads, values_part)
    dscore = probs * (dprob - jnp.sum(probs * dprob, axis=-1, keepdims=True)) * (HEAD ** -0.5)
    dscore_b = dscore.astype(jnp.bfloat16).astype(jnp.float32)
    grad_q = jnp.einsum("hqk,khd->qhd", dscore_b, keys_part)
    grad_k = jnp.einsum("hqk,qhd->khd", dscore_b, queries)
    grad_v = jnp.einsum("hqk,qhd->khd", probs_b.astype(jnp.float32), grads)
    stacked = jnp.stack([grad_q, grad_k, grad_v], axis=1)
    return stacked.reshape(row_count, 3, head_count * HEAD).astype(jnp.bfloat16)


def reference(qkv_rows, out_weight, out_grad, image_len, dest_rank, dest_offset):
    image_lens = image_len.reshape(N_DP, SLOTS)
    dest_table = dest_rank.reshape(N_DP, SLOTS)
    offset_table = dest_offset.reshape(N_DP, SLOTS)
    start_table = jnp.cumsum(image_lens, axis=1) - image_lens
    positions = jnp.arange(HOME, dtype=jnp.int32)
    slot_ids = jnp.arange(SLOTS, dtype=jnp.int32)
    inside = (positions[None, :, None] >= start_table[:, None, :]) & (positions[None, :, None] < (start_table + image_lens)[:, None, :])
    home_valid = jnp.any(inside, axis=-1)
    seg_table = jnp.where(home_valid, jnp.sum(jnp.where(inside, slot_ids[None, None, :], 0), axis=-1), -1).astype(jnp.int32)
    work_row = jnp.sum(jnp.where(inside, dest_table[:, None, :] * CAP + offset_table[:, None, :] + positions[None, :, None] - start_table[:, None, :], 0), axis=-1)
    target = jnp.where(home_valid, work_row, N_DP * CAP).reshape(-1).astype(jnp.int32)
    blocks = qkv_rows.reshape(N_DP, HOME, 3, INNER)
    att_home = lax.map(lambda block_args: attend(block_args[0], block_args[1])[0], (blocks, seg_table))
    att_work = jnp.zeros((N_DP * CAP, INNER), jnp.bfloat16).at[target].set(att_home.reshape(-1, INNER), mode="drop")
    slice_width = INNER // N_MP
    mixed = jnp.zeros((N_DP * CAP, D), jnp.float32)
    for slice_id in range(N_MP):
        term = jnp.dot(att_work[:, slice_id * slice_width:(slice_id + 1) * slice_width], out_weight[slice_id * slice_width:(slice_id + 1) * slice_width], preferred_element_type=jnp.float32)
        rounded = lax.optimization_barrier(term.astype(jnp.bfloat16))
        mixed = mixed + rounded.astype(jnp.float32)
    mixed = mixed.astype(jnp.bfloat16)
    att_grad_work = jnp.dot(out_grad, out_weight.T, preferred_element_type=jnp.float32).astype(jnp.bfloat16)
    work_blocks = att_work.reshape(N_DP, CAP, INNER)
    grad_blocks = out_grad.reshape(N_DP, CAP, D)

    def add_rank(total, pair):
        term = jnp.dot(pair[0].T, pair[1], preferred_element_type=jnp.float32)
        rounded = lax.optimization_barrier(term.astype(jnp.bfloat16))
        return total + rounded.astype(jnp.float32), None

    weight_sum, unused = lax.scan(add_rank, jnp.zeros((INNER, D), jnp.float32), (work_blocks, grad_blocks))
    weight_grad = weight_sum.astype(jnp.bfloat16)
    taken = jnp.take(att_grad_work, jnp.clip(target, 0, N_DP * CAP - 1), axis=0)
    att_grad = jnp.where(home_valid.reshape(-1)[:, None], taken, jnp.zeros_like(taken)).reshape(N_DP, HOME, INNER)
    grads = lax.map(lambda block_args: attend_back(block_args[0], block_args[1], block_args[2]), (blocks, seg_table, att_grad))
    return mixed, grads.reshape(N_DP * HOME, 3, INNER), weight_grad
```

```python
import functools

import jax
import jax.numpy as jnp
from jax import lax
from jax.experimental import pallas as pl
from jax.experimental.pallas import tpu as pltpu
from jax.sharding import PartitionSpec as P

HEAD = 128
UNIT = 64
SLOTS = 8
NZ, NX, NY = 8, 4, 4
NDP = NZ * NX
HOME = 512
CAP = 384
HEADS = 3
INN = HEADS * HEAD
COLS = 768
DOWN = 1 / HEAD ** 0.5
MESH = pl.DeviceIdType.MESH
F32 = jnp.float32
BF = jnp.bfloat16
HALF = CAP // 2
RX = 256
RZ = 128
PX = RX // NX
PZ = RZ // NX
WINDOWS = ((0, 384), (0, 512), (0, 512), (128, 512))


def add(a, b):
    return (a.astype(F32) + b.astype(F32)).astype(BF)


def nt(a, b):
    return lax.dot_general(a, b, (((1,), (1,)), ((), ())), preferred_element_type=F32)


def nn(a, b):
    return jnp.dot(a, b, preferred_element_type=F32)


def kernel(len_ref, dest_ref, qkv_hbm, w_hbm, g_hbm, mixed_ref, dqkv_ref, wg_ref,
           qkv, w, gb, bias, probs, att_home, att_send, att_recv, att, att_t, acc, agw, back_recv,
           ghome, dk_t, dv_t, wt1, wt2, psend, precv, rbuf, yrp, yrm, xlp, xlm, xrp, xrm, xr,
           z1p, z1m, z2p, z2m, zr2, x2p, x2m, wfin, wrecv, ss, rs, ls):
    dp, mp = lax.axis_index("dp"), lax.axis_index("mp")
    z, x = lax.div(dp, NX), lax.rem(dp, NX)
    y, c = lax.div(mp, 2), lax.rem(mp, 2)

    def at_y(d):
        return lax.rem(y + d + NY, NY)

    def at_x(d):
        return lax.rem(x + d + NX, NX)

    def at_z(d):
        return lax.rem(z + d + NZ, NZ)

    def at_dp(d):
        return lax.rem(dp + d + NDP, NDP)

    sib = (dp, 2 * y + 1 - c)
    yp, ym = (dp, 2 * at_y(1) + c), (dp, 2 * at_y(-1) + c)
    xp, xm, xo = (z * NX + at_x(1), mp), (z * NX + at_x(-1), mp), (z * NX + at_x(2), mp)
    zp, zm = (at_z(1) * NX + x, mp), (at_z(-1) * NX + x, mp)
    nxt, prv, acr = (at_dp(1), mp), (at_dp(-1), mp), (at_dp(NDP // 2), mp)
    partners = (sib, yp, ym, xp, xm, xo, zp, zm, nxt, prv, acr)

    in_g = pltpu.make_async_copy(g_hbm, gb.at[0], ls.at[0])
    in_qkv = pltpu.make_async_copy(qkv_hbm, qkv, ls.at[1])
    in_w = pltpu.make_async_copy(w_hbm, w, ls.at[2])
    in_g.start()
    in_qkv.start()
    in_w.start()

    barrier = pltpu.get_barrier_semaphore()
    for one in partners:
        pl.semaphore_signal(barrier, inc=1, device_id=one, device_id_type=MESH)
    pl.semaphore_wait(barrier, len(partners))

    sent = []

    def send(src, dst, to):
        i = len(sent)
        copy = pltpu.make_async_remote_copy(
            src_ref=src, dst_ref=dst, send_sem=ss.at[i], recv_sem=rs.at[i], device_id=to,
            device_id_type=MESH)
        copy.start()
        sent.append(copy)
        return copy

    top, bot = pl.ds(0, HALF), pl.ds(HALF, HALF)

    in_g.wait()
    g_yp_top = send(gb.at[0, top], gb.at[2, top], yp)
    g_ym_bot = send(gb.at[0, bot], gb.at[3, bot], ym)
    g_yp_bot = send(gb.at[0, bot], gb.at[2, bot], yp)
    g_ym_top = send(gb.at[0, top], gb.at[3, top], ym)
    g_sib = send(gb.at[0], gb.at[1], sib)

    def ends_of(rank):
        ends, total = [], jnp.int32(0)
        for s in range(SLOTS):
            total = total + len_ref[rank * SLOTS + s]
            ends.append(total)
        return ends

    ends = ends_of(dp)

    def moved(rank, slot):
        return (dest_ref[rank * SLOTS + slot] != rank) & (len_ref[rank * SLOTS + slot] > 0)

    def image_of(pos):
        out = jnp.zeros(pos.shape, jnp.int32)
        for end in ends:
            out = out + (pos >= end).astype(jnp.int32)
        return out

    rows_at = image_of(lax.broadcasted_iota(jnp.int32, (HOME, 1), 0))
    cols_at = image_of(lax.broadcasted_iota(jnp.int32, (1, HOME), 1))
    bias[...] = jnp.where(rows_at == cols_at, 0.0, -1e30).astype(F32)

    in_qkv.wait()

    def forward(h, carry):
        at = pl.multiple_of(h * HEAD, HEAD)
        for i, (lo, hi) in enumerate(WINDOWS):
            rows, keys = pl.ds(i * 128, 128), pl.ds(lo, hi - lo)
            q = qkv[rows, pl.ds(at, HEAD)]
            k = qkv[keys, pl.ds(at + INN, HEAD)]
            v = qkv[keys, pl.ds(at + 2 * INN, HEAD)]
            s = nt(q, k) * DOWN + bias[rows, keys]
            e = jnp.exp(s - jnp.max(s, axis=-1, keepdims=True))
            p = e / jnp.sum(e, axis=-1, keepdims=True)
            probs[h, rows, keys] = p
            att_home[rows, pl.ds(at, HEAD)] = nn(p.astype(BF), v).astype(BF)
        return carry

    lax.fori_loop(0, HEADS, forward, 0)

    def unit(ref, u):
        return ref[pl.ds(u * UNIT, UNIT), :].astype(F32)

    starts = [jnp.int32(0)] + ends[:-1]
    for i, slot in enumerate((6, 7, 5)):
        pick = jnp.where(starts[slot] == 5 * UNIT, unit(att_home, 5),
                         jnp.where(starts[slot] == 6 * UNIT, unit(att_home, 6), unit(att_home, 7)))
        att_send[i] = pick.astype(BF)
    moves = [send(att_send.at[i], att_recv.at[i], to) for i, to in enumerate((nxt, prv, acr))]

    g_yp_top.wait_recv()
    g_yo_top = send(gb.at[2, top], gb.at[6, top], yp)
    g_sib_4t = send(gb.at[2, top], gb.at[4, top], sib)
    g_ym_bot.wait_recv()
    g_yo_bot = send(gb.at[3, bot], gb.at[6, bot], ym)
    g_sib_5b = send(gb.at[3, bot], gb.at[5, bot], sib)

    for m in moves:
        m.wait_recv()
    from_prv, from_nxt, from_acr = moved(at_dp(-1), 6), moved(at_dp(1), 7), moved(at_dp(NDP // 2), 5)
    last = jnp.where(from_prv, att_recv[0].astype(F32),
                     jnp.where(from_nxt, att_recv[1].astype(F32),
                               jnp.where(from_acr, att_recv[2].astype(F32), unit(att_home, 5))))
    att[pl.ds(0, 5 * UNIT), :] = att_home[pl.ds(0, 5 * UNIT), :]
    att[pl.ds(5 * UNIT, UNIT), :] = last.astype(BF)
    att_t[...] = att[...].astype(F32).T.astype(BF)

    def flip_of(f):
        return c + f - 2 * c * f

    def first_group(j):
        return 2 * y + flip_of(j)

    def second_group(j):
        i = j - 2
        return 2 * at_y(2 * lax.rem(i, 2) - 1) + flip_of(lax.div(i, 2))

    def third_group(j):
        return 2 * at_y(2) + flip_of(j - 6)

    in_w.wait()
    acc[...] = jnp.zeros_like(acc)

    def cols_of(block):
        return pl.ds(pl.multiple_of(block * COLS, COLS), COLS)

    def terms(lo, hi, block_of):
        def one(j, carry):
            block = block_of(j)
            t = nn(att_t[...], gb[j]).astype(BF)
            wt1[j] = t[:RX]
            wt2[block] = t[RX:]
            return carry

        lax.fori_loop(lo, hi, one, 0)

    def grads(lo, hi, block_of):
        def one(j, carry):
            acc[...] += nt(gb[j], w[:, cols_of(block_of(j))])
            return carry

        lax.fori_loop(lo, hi, one, 0)

    def along_x(lo, half, block_of):
        far, right, left = (pl.ds(pl.multiple_of(at_x(d) * PX, PX), PX) for d in (2, 1, -1))
        mine = pl.ds(pl.multiple_of(x * PX, PX), PX)
        a, b = pl.ds(lo, half), pl.ds(lo + half, half)
        la = pl.ds(lo // 2, half)
        relay_p = send(wt1.at[a, far], xlp.at[la], xp)
        relay_m = send(wt1.at[b, far], xlm.at[la], xm)
        early_p = send(wt1.at[b, right], xrp.at[b], xp)
        early_m = send(wt1.at[a, left], xrm.at[a], xm)
        yield
        relay_p.wait_recv()
        for i in range(half):
            wt1[lo + i, right] = add(wt1[lo + i, right], xlp[lo // 2 + i])
        late_p = send(wt1.at[a, right], xrp.at[a], xp)
        relay_m.wait_recv()
        for i in range(half):
            wt1[lo + half + i, left] = add(wt1[lo + half + i, left], xlm[lo // 2 + i])
        late_m = send(wt1.at[b, left], xrm.at[b], xm)
        yield
        for copy in (early_p, early_m, late_p, late_m):
            copy.wait_recv()

        def one(j, carry):
            total = wt1[j, mine].astype(F32) + xrp[j].astype(F32) + xrm[j].astype(F32)
            xr[block_of(j)] = total.astype(BF)
            return carry

        lax.fori_loop(lo, lo + 2 * half, one, 0)
        yield

    def along_z(buf, rows, from_m, from_p, out):
        half = rows // 2
        up, down = pl.ds(0, half), pl.ds(half, half)
        a = send(buf.at[at_z(4), up], from_m.at[3, up], zp)
        b = send(buf.at[at_z(4), down], from_p.at[3, down], zm)
        yield
        for d in (3, 2, 1):
            part_a, part_b = (up, down) if d == 3 else (slice(None), slice(None))
            a.wait_recv()
            here = at_z(d)
            buf[here, part_a] = add(buf[here, part_a], from_m[d, part_a])
            a = send(buf.at[here], from_m.at[d - 1], zp)
            b.wait_recv()
            here = at_z(-d)
            buf[here, part_b] = add(buf[here, part_b], from_p[d, part_b])
            b = send(buf.at[here], from_p.at[d - 1], zm)
            yield
        a.wait_recv()
        b.wait_recv()
        out[...] = (buf[z].astype(F32) + from_m[0].astype(F32) + from_p[0].astype(F32)).astype(BF)
        yield

    def along_x_last():
        far, right, left, mine = (pl.multiple_of(at_x(d) * PZ, PZ) for d in (2, 1, -1, 0))
        half = PZ // 2
        up, down = pl.ds(0, half), pl.ds(half, half)
        a = send(zr2.at[pl.ds(far, half)], x2p.at[1, up], xp)
        b = send(zr2.at[pl.ds(pl.multiple_of(far + half, half), half)], x2m.at[1, down], xm)
        yield
        a.wait_recv()
        zr2[pl.ds(right, half)] = add(zr2[pl.ds(right, half)], x2p[1, up])
        a = send(zr2.at[pl.ds(right, PZ)], x2p.at[0], xp)
        b.wait_recv()
        low = pl.ds(pl.multiple_of(left + half, half), half)
        zr2[low] = add(zr2[low], x2m[1, down])
        b = send(zr2.at[pl.ds(left, PZ)], x2m.at[0], xm)
        yield
        a.wait_recv()
        b.wait_recv()
        total = zr2[pl.ds(mine, PZ)].astype(F32) + x2p[0].astype(F32) + x2m[0].astype(F32)
        wfin[pl.ds(PX, PZ)] = total.astype(BF)
        yield

    g_sib.wait_recv()
    terms(0, 2, first_group)
    x1 = along_x(0, 1, first_group)
    next(x1)

    turns = (2, 1, -1, 0)

    def turn(i):
        return lax.rem(y + 2 + 3 * i, NY)

    p_base = len(sent)

    def p_copy(i):
        return pltpu.make_async_remote_copy(
            src_ref=psend.at[i], dst_ref=precv.at[i], send_sem=ss.at[p_base + i],
            recv_sem=rs.at[p_base + i], device_id=sib, device_id_type=MESH)

    def for_sibling(i, carry):
        psend[i] = nn(att[...], w[:, cols_of(2 * turn(i) + 1 - c)]).astype(BF)
        p_copy(i).start()
        return carry

    lax.fori_loop(0, NY, for_sibling, 0)
    sent.extend(p_copy(i) for i in range(NY))

    def for_me(i, carry):
        rbuf[i] = nn(att[...], w[:, cols_of(2 * turn(i) + c)]).astype(BF)
        return carry

    lax.fori_loop(0, NY, for_me, 0)
    next(x1)

    def merge(i):
        sent[p_base + i].wait_recv()
        rbuf[i] = add(rbuf[i], precv[i])

    merge(0)
    r_far_p = send(rbuf.at[0, top], yrp.at[1, top], yp)
    r_far_m = send(rbuf.at[0, bot], yrm.at[1, bot], ym)
    merge(1)
    r_yp_bot = send(rbuf.at[1, bot], yrp.at[0, bot], yp)
    merge(3)
    r_ym_top = send(rbuf.at[3, top], yrm.at[0, top], ym)
    merge(2)

    grads(0, 2, first_group)

    g_yp_bot.wait_recv()
    g_sib_4b = send(gb.at[2, bot], gb.at[4, bot], sib)
    g_ym_top.wait_recv()
    g_sib_5t = send(gb.at[3, top], gb.at[5, top], sib)
    next(x1)
    for copy in (g_sib_4t, g_sib_4b, g_sib_5t, g_sib_5b):
        copy.wait_recv()
    terms(2, 6, second_group)
    x2 = along_x(2, 2, second_group)
    next(x2)
    grads(2, 6, second_group)

    g_yo_top.wait_recv()
    g_sib_7t = send(gb.at[6, top], gb.at[7, top], sib)
    g_yo_bot.wait_recv()
    g_sib_7b = send(gb.at[6, bot], gb.at[7, bot], sib)
    next(x2)
    g_sib_7t.wait_recv()
    g_sib_7b.wait_recv()
    terms(6, 8, third_group)
    x3 = along_x(6, 1, third_group)
    next(x3)
    z2 = along_z(wt2, RZ, z2p, z2m, zr2)
    next(z2)
    grads(6, 8, third_group)
    agw[...] = acc[...].astype(BF)
    tail = agw.at[pl.ds(5 * UNIT, UNIT)]
    backs = [send(tail, back_recv.at[i], to) for i, to in enumerate((prv, nxt, acr))]

    r_far_p.wait_recv()
    rbuf[1, top] = add(rbuf[1, top], yrp[1, top])
    r_yp_top = send(rbuf.at[1, top], yrp.at[0, top], yp)
    r_far_m.wait_recv()
    rbuf[3, bot] = add(rbuf[3, bot], yrm[1, bot])
    r_ym_bot = send(rbuf.at[3, bot], yrm.at[0, bot], ym)
    next(x2)

    for copy in backs:
        copy.wait_recv()
    got = from_prv | from_nxt | from_acr
    ghome[pl.ds(0, 5 * UNIT), :] = agw[pl.ds(0, 5 * UNIT), :]
    for u in (5, 6, 7):
        value = jnp.zeros((UNIT, INN), F32)
        for i, slot in enumerate((6, 7, 5)):
            hit = moved(dp, slot) & (starts[slot] == u * UNIT)
            value = jnp.where(hit, back_recv[i].astype(F32), value)
        if u == 5:
            value = jnp.where(got, value, unit(agw, 5))
        ghome[pl.ds(u * UNIT, UNIT), :] = value.astype(BF)

    def backward(h, carry):
        at = pl.multiple_of(h * HEAD, HEAD)
        q_t = qkv[:, pl.ds(at, HEAD)].astype(F32).T.astype(BF)
        g_t = ghome[:, pl.ds(at, HEAD)].astype(F32).T.astype(BF)
        dk_t[...] = jnp.zeros_like(dk_t)
        dv_t[...] = jnp.zeros_like(dv_t)
        for i, (lo, hi) in enumerate(WINDOWS):
            rows, keys = pl.ds(i * 128, 128), pl.ds(lo, hi - lo)
            k = qkv[keys, pl.ds(at + INN, HEAD)]
            v = qkv[keys, pl.ds(at + 2 * INN, HEAD)]
            p = probs[h, rows, keys]
            dp_ = nt(ghome[rows, pl.ds(at, HEAD)], v)
            mean = jnp.sum(p * dp_, axis=-1, keepdims=True)
            ds = (p * (dp_ - mean) * DOWN).astype(BF)
            dqkv_ref[rows, pl.ds(at, HEAD)] = nn(ds, k).astype(BF)
            mine = slice(i * 128, (i + 1) * 128)
            dk_t[:, keys] += nn(q_t[:, mine], ds)
            dv_t[:, keys] += nn(g_t[:, mine], p.astype(BF))
        dqkv_ref[:, pl.ds(at + INN, HEAD)] = dk_t[...].T.astype(BF)
        dqkv_ref[:, pl.ds(at + 2 * INN, HEAD)] = dv_t[...].T.astype(BF)
        return carry

    next(x3)
    next(z2)
    lax.fori_loop(0, 1, backward, 0)
    next(x3)
    z1 = along_z(xr, PX, z1p, z1m, wfin.at[pl.ds(0, PX)])
    next(z1)
    next(z2)
    lax.fori_loop(1, 2, backward, 0)
    next(z1)
    next(z2)
    lax.fori_loop(2, 3, backward, 0)
    next(z1)
    next(z2)
    xl = along_x_last()
    next(xl)
    next(z1)
    next(xl)
    next(z1)
    next(xl)

    def window(at):
        return pl.ds(pl.multiple_of(lax.div(at, 2) * 384 + lax.rem(at, 2) * 128, 128), 256)

    lasts = [send(wfin.at[:, window(at_x(d))], wrecv.at[i], to)
             for i, (d, to) in enumerate(((1, xp), (-1, xm), (2, xo)))]

    def place(of, rows):
        wg_ref[pl.ds(pl.multiple_of(of * PX, PX), PX), :] = rows[:PX]
        wg_ref[pl.ds(pl.multiple_of(RX + of * PZ, PZ), PZ), :] = rows[PX:]

    for copy in (r_yp_bot, r_yp_top, r_ym_top, r_ym_bot):
        copy.wait_recv()
    mixed_ref[...] = (rbuf[2].astype(F32) + yrp[0].astype(F32) + yrm[0].astype(F32)).astype(BF)

    place(x, wfin[:, window(x)])
    for i, d in enumerate((-1, 1, 2)):
        lasts[i].wait_recv()
        place(at_x(d), wrecv[i])
    for copy in sent:
        copy.wait_send()


def scratch():
    v = pltpu.VMEM
    return [
        v((HOME, 3 * INN), BF), v((INN, 8 * COLS), BF), v((8, CAP, COLS), BF), v((HOME, HOME), F32),
        v((HEADS, HOME, HOME), F32), v((HOME, INN), BF), v((3, UNIT, INN), BF), v((3, UNIT, INN), BF),
        v((CAP, INN), BF), v((INN, CAP), BF), v((CAP, INN), F32), v((CAP, INN), BF), v((3, UNIT, INN), BF),
        v((HOME, INN), BF), v((HEAD, HOME), F32), v((HEAD, HOME), F32),
        v((8, RX, COLS), BF), v((8, RZ, COLS), BF),
        v((4, CAP, COLS), BF), v((4, CAP, COLS), BF), v((4, CAP, COLS), BF),
        v((2, CAP, COLS), BF), v((2, CAP, COLS), BF),
        v((4, PX, COLS), BF), v((4, PX, COLS), BF), v((8, PX, COLS), BF), v((8, PX, COLS), BF),
        v((8, PX, COLS), BF),
        v((4, PX, COLS), BF), v((4, PX, COLS), BF), v((4, RZ, COLS), BF), v((4, RZ, COLS), BF),
        v((RZ, COLS), BF), v((2, PZ, COLS), BF), v((2, PZ, COLS), BF),
        v((PX + PZ, COLS), BF), v((3, PX + PZ, 256), BF),
        pltpu.SemaphoreType.DMA((96,)), pltpu.SemaphoreType.DMA((96,)), pltpu.SemaphoreType.DMA((3,)),
    ]


def body(qkv_rows, out_weight, out_grad, image_len, dest_rank, dest_offset):
    smem = pl.BlockSpec(memory_space=pltpu.SMEM)
    anywhere = pl.BlockSpec(memory_space=pl.ANY)
    vmem = pl.BlockSpec(memory_space=pltpu.VMEM)
    mixed, dqkv, wide = pl.pallas_call(
        kernel,
        out_shape=(
            jax.ShapeDtypeStruct((CAP, COLS), BF),
            jax.ShapeDtypeStruct((HOME, 3 * INN), BF),
            jax.ShapeDtypeStruct((INN, 256), BF),
        ),
        in_specs=[smem, smem, anywhere, anywhere, anywhere],
        out_specs=(vmem, vmem, vmem),
        scratch_shapes=scratch(),
        compiler_params=pltpu.CompilerParams(
            collective_id=0, has_side_effects=True, vmem_limit_bytes=60 * 2**20),
    )(image_len, dest_rank, qkv_rows.reshape(HOME, 3 * INN), out_weight, out_grad)
    odd = lax.rem(lax.axis_index("dp"), 2)
    weight_grad = lax.dynamic_slice_in_dim(wide, odd * 64, 192, axis=1)
    return mixed, dqkv.reshape(HOME, 3, INN), weight_grad


def solution(mesh):
    return jax.shard_map(
        body,
        mesh=mesh,
        in_specs=(P("dp", None, "mp"), P("mp", None), P("dp", "mp"), P(), P(), P()),
        out_specs=(P("dp", "mp"), P("dp", None, "mp"), P("mp", "dp")),
        check_vma=False,
    )
```

```python
import functools

import jax
import jax.numpy as jnp
from jax import lax
from jax.experimental import pallas as pl
from jax.experimental.pallas import tpu as pltpu
from jax.sharding import PartitionSpec as P

HEAD = 128
UNIT = 64
SLOTS = 8
NZ, NX, NY = 8, 4, 4
NDP = NZ * NX
HOME = 512
CAP = 384
HEADS = 3
INN = HEADS * HEAD
COLS = 768
DOWN = 1 / HEAD ** 0.5
MESH = pl.DeviceIdType.MESH
F32 = jnp.float32
BF = jnp.bfloat16
HALF = CAP // 2
LX = 256
LZ = INN - LX
PART = COLS // NX
ZROWS = 384
XROWS = 96
QUARTER = CAP // 4
WINDOWS = ((0, 384), (0, 512), (0, 512), (128, 512))


ORDER = (
    "P", "S", "F", "Q", "X1", "N", "T2A", "A", "T2B", "C", "M", "A", "X1", "W", "YF", "YE", "T3A", "T3B",
    "Z2", "X3", "C", "A", "G2", "Z2", "G3", "BK", "YL", "C", "X3", "Z2", "HM", "B0", "X3", "Z1", "Z2",
    "B1", "Z1", "Z2", "XL", "Z1", "B2", "XL", "Z1", "XL", "YD", "Z1",
)


def add(a, b):
    return (a.astype(F32) + b.astype(F32)).astype(BF)


def nt(a, b):
    return lax.dot_general(a, b, (((1,), (1,)), ((), ())), preferred_element_type=F32)


def nn(a, b):
    return jnp.dot(a, b, preferred_element_type=F32)


def kernel(len_ref, dest_ref, qkv_hbm, w_hbm, g_hbm, mixed_hbm, dqkv_hbm, wg_hbm,
           qkv, w, gb, bias, probs, att_home, att_send, att_recv, att, acc, agw, back_recv,
           ghome, dk_t, dv_t, wt1, wt2, psend, precv, rbuf, yrp, yrm, xlp, xlm, xrp, xrm, xr,
           z1p, z1m, z2p, z2m, zr2, x2p, x2m, mixed, dqkv, wg, ss, rs, ls):
    dp, mp = lax.axis_index("dp"), lax.axis_index("mp")
    z, x = lax.div(dp, NX), lax.rem(dp, NX)
    y, c = lax.div(mp, 2), lax.rem(mp, 2)

    def at_y(d):
        return lax.rem(y + d + NY, NY)

    def at_x(d):
        return lax.rem(x + d + NX, NX)

    def at_z(d):
        return lax.rem(z + d + NZ, NZ)

    def at_dp(d):
        return lax.rem(dp + d + NDP, NDP)

    sib = (dp, 2 * y + 1 - c)
    yp, ym = (dp, 2 * at_y(1) + c), (dp, 2 * at_y(-1) + c)
    xp, xm = (z * NX + at_x(1), mp), (z * NX + at_x(-1), mp)
    zp, zm = (at_z(1) * NX + x, mp), (at_z(-1) * NX + x, mp)
    nxt, prv, acr = (at_dp(1), mp), (at_dp(-1), mp), (at_dp(NDP // 2), mp)
    partners = (sib, yp, ym, xp, xm, zp, zm, nxt, prv, acr)

    in_g = pltpu.make_async_copy(g_hbm, gb.at[0], ls.at[0])
    in_qkv = pltpu.make_async_copy(qkv_hbm, qkv, ls.at[1])
    in_w = pltpu.make_async_copy(w_hbm, w, ls.at[2])
    out_mixed = pltpu.make_async_copy(mixed, mixed_hbm, ls.at[3])
    out_dqkv = pltpu.make_async_copy(dqkv, dqkv_hbm, ls.at[4])
    out_wg = pltpu.make_async_copy(wg, wg_hbm, ls.at[5])
    in_g.start()
    in_qkv.start()
    in_w.start()

    barrier = pltpu.get_barrier_semaphore()
    for one in partners:
        pl.semaphore_signal(barrier, inc=1, device_id=one, device_id_type=MESH)
    pl.semaphore_wait(barrier, len(partners))

    sent = []

    def send(src, dst, to):
        i = len(sent)
        copy = pltpu.make_async_remote_copy(
            src_ref=src, dst_ref=dst, send_sem=ss.at[i], recv_sem=rs.at[i], device_id=to,
            device_id_type=MESH)
        copy.start()
        sent.append(copy)
        return copy

    top, bot = pl.ds(0, HALF), pl.ds(HALF, HALF)

    in_g.wait()
    quarters = [pl.ds(i * QUARTER, QUARTER) for i in range(4)]
    first, later = {}, {}
    for i in range(2):
        first[i] = (send(gb.at[0, quarters[i]], gb.at[2, quarters[i]], yp),
                    send(gb.at[0, quarters[i + 2]], gb.at[3, quarters[i + 2]], ym))
    g_sib = send(gb.at[0], gb.at[1], sib)

    def ends_of(rank):
        ends, total = [], jnp.int32(0)
        for s in range(SLOTS):
            total = total + len_ref[rank * SLOTS + s]
            ends.append(total)
        return ends

    ends = ends_of(dp)

    def moved(rank, slot):
        return (dest_ref[rank * SLOTS + slot] != rank) & (len_ref[rank * SLOTS + slot] > 0)

    def image_of(pos):
        out = jnp.zeros(pos.shape, jnp.int32)
        for end in ends:
            out = out + (pos >= end).astype(jnp.int32)
        return out

    rows_at = image_of(lax.broadcasted_iota(jnp.int32, (HOME, 1), 0))
    cols_at = image_of(lax.broadcasted_iota(jnp.int32, (1, HOME), 1))
    bias[...] = jnp.where(rows_at == cols_at, 0.0, -1e30).astype(F32)

    in_qkv.wait()

    def forward(h, carry):
        at = pl.multiple_of(h * HEAD, HEAD)
        for i, (lo, hi) in enumerate(WINDOWS):
            rows, keys = pl.ds(i * 128, 128), pl.ds(lo, hi - lo)
            q = qkv[0, rows, pl.ds(at, HEAD)]
            k = qkv[1, keys, pl.ds(at, HEAD)]
            v = qkv[2, keys, pl.ds(at, HEAD)]
            s = nt(q, k) * DOWN + bias[rows, keys]
            e = jnp.exp(s - jnp.max(s, axis=-1, keepdims=True))
            p = e / jnp.sum(e, axis=-1, keepdims=True)
            probs[h, rows, keys] = p
            att_home[rows, pl.ds(at, HEAD)] = nn(p.astype(BF), v).astype(BF)
        return carry

    lax.fori_loop(0, HEADS, forward, 0)
    for i in range(2):
        later[i] = (send(gb.at[0, quarters[i + 2]], gb.at[2, quarters[i + 2]], yp),
                    send(gb.at[0, quarters[i]], gb.at[3, quarters[i]], ym))

    def unit(ref, u):
        return ref[pl.ds(u * UNIT, UNIT), :].astype(F32)

    starts = [jnp.int32(0)] + ends[:-1]
    for i, slot in enumerate((6, 7, 5)):
        pick = jnp.where(starts[slot] == 5 * UNIT, unit(att_home, 5),
                         jnp.where(starts[slot] == 6 * UNIT, unit(att_home, 6), unit(att_home, 7)))
        att_send[i] = pick.astype(BF)
    moves = [send(att_send.at[i], att_recv.at[i], to) for i, to in enumerate((nxt, prv, acr))]

    def flip_of(f):
        return c + f - 2 * c * f

    def first_group(j):
        return 2 * y + flip_of(j)

    def second_group(j):
        i = j - 2
        return 2 * at_y(2 * lax.rem(i, 2) - 1) + flip_of(lax.div(i, 2))

    def third_group(j):
        return 2 * at_y(2) + flip_of(j - 6)

    def cols_of(block):
        return pl.ds(pl.multiple_of(block * COLS, COLS), COLS)

    def terms(lo, hi, block_of):
        def one(j, carry):
            t = lax.dot_general(gb[j], att[...], (((0,), (0,)), ((), ())),
                                preferred_element_type=F32).astype(BF)
            wt1[j] = t[:, :LX]
            wt2[block_of(j)] = t[:, LX:]
            return carry

        lax.fori_loop(lo, hi, one, 0)

    def grads(lo, hi, block_of):
        def one(j, carry):
            acc[...] += nt(gb[j], w[:, cols_of(block_of(j))])
            return carry

        lax.fori_loop(lo, hi, one, 0)

    def along_x(lo, half, block_of):
        far, right, left = (pl.ds(pl.multiple_of(at_x(d) * PART, PART), PART) for d in (2, 1, -1))
        mine = pl.ds(pl.multiple_of(x * PART, PART), PART)
        a, b = pl.ds(lo, half), pl.ds(lo + half, half)
        la = pl.ds(lo // 2, half)
        relay_p = send(wt1.at[a, far], xlp.at[la], xp)
        relay_m = send(wt1.at[b, far], xlm.at[la], xm)
        early_p = send(wt1.at[b, right], xrp.at[b], xp)
        early_m = send(wt1.at[a, left], xrm.at[a], xm)
        yield
        relay_p.wait_recv()
        for i in range(half):
            wt1[lo + i, right] = add(wt1[lo + i, right], xlp[lo // 2 + i])
        late_p = send(wt1.at[a, right], xrp.at[a], xp)
        relay_m.wait_recv()
        for i in range(half):
            wt1[lo + half + i, left] = add(wt1[lo + half + i, left], xlm[lo // 2 + i])
        late_m = send(wt1.at[b, left], xrm.at[b], xm)
        yield
        for copy in (early_p, early_m, late_p, late_m):
            copy.wait_recv()

        def one(j, carry):
            total = wt1[j, mine].astype(F32) + xrp[j].astype(F32) + xrm[j].astype(F32)
            xr[block_of(j)] = total.astype(BF)
            return carry

        lax.fori_loop(lo, lo + 2 * half, one, 0)
        yield

    def along_z(buf, first, rows, from_m, from_p, out, lanes):
        half = rows // 2
        up, down, both = pl.ds(first, half), pl.ds(first + half, half), pl.ds(first, rows)
        a = send(buf.at[at_z(4), up], from_m.at[3, up], zp)
        b = send(buf.at[at_z(4), down], from_p.at[3, down], zm)
        yield
        for d in (3, 2, 1):
            part_a, part_b = (up, down) if d == 3 else (both, both)
            a.wait_recv()
            here = at_z(d)
            buf[here, part_a] = add(buf[here, part_a], from_m[d, part_a])
            a = send(buf.at[here, both], from_m.at[d - 1, both], zp)
            b.wait_recv()
            here = at_z(-d)
            buf[here, part_b] = add(buf[here, part_b], from_p[d, part_b])
            b = send(buf.at[here, both], from_p.at[d - 1, both], zm)
            yield
        a.wait_recv()
        b.wait_recv()
        total = buf[z, both].astype(F32) + from_m[0, both].astype(F32) + from_p[0, both].astype(F32)
        out[both, lanes] = total.astype(BF)
        yield

    def along_x_last():
        far, right, left, mine = (pl.multiple_of(at_x(d) * PART, PART) for d in (2, 1, -1, 0))
        half = PART // 2
        up, down = pl.ds(0, half), pl.ds(half, half)
        a = send(zr2.at[pl.ds(far, half)], x2p.at[1, up], xp)
        b = send(zr2.at[pl.ds(pl.multiple_of(far + half, half), half)], x2m.at[1, down], xm)
        yield
        a.wait_recv()
        zr2[pl.ds(right, half)] = add(zr2[pl.ds(right, half)], x2p[1, up])
        a = send(zr2.at[pl.ds(right, PART)], x2p.at[0], xp)
        b.wait_recv()
        low = pl.ds(pl.multiple_of(left + half, half), half)
        zr2[low] = add(zr2[low], x2m[1, down])
        b = send(zr2.at[pl.ds(left, PART)], x2m.at[0], xm)
        yield
        a.wait_recv()
        b.wait_recv()
        total = zr2[pl.ds(mine, PART)].astype(F32) + x2p[0].astype(F32) + x2m[0].astype(F32)
        wg[:, LX:] = total.astype(BF)
        yield

    in_w.wait()
    acc[...] = jnp.zeros_like(acc)
    g_sib.wait_recv()
    grads(0, 2, first_group)

    for m in moves:
        m.wait_recv()
    from_prv, from_nxt, from_acr = moved(at_dp(-1), 6), moved(at_dp(1), 7), moved(at_dp(NDP // 2), 5)
    last = jnp.where(from_prv, att_recv[0].astype(F32),
                     jnp.where(from_nxt, att_recv[1].astype(F32),
                               jnp.where(from_acr, att_recv[2].astype(F32), unit(att_home, 5))))
    att[pl.ds(0, 5 * UNIT), :] = att_home[pl.ds(0, 5 * UNIT), :]
    att[pl.ds(5 * UNIT, UNIT), :] = last.astype(BF)

    terms(0, 2, first_group)
    x1 = along_x(0, 1, first_group)
    next(x1)

    def turn(i):
        return lax.rem(y + 2 + 3 * i, NY)

    p_base = len(sent)

    def p_copy(i):
        return pltpu.make_async_remote_copy(
            src_ref=psend.at[i], dst_ref=precv.at[i], send_sem=ss.at[p_base + i],
            recv_sem=rs.at[p_base + i], device_id=sib, device_id_type=MESH)

    sent.extend(p_copy(i) for i in range(NY))

    def for_sibling():
        def one(i, carry):
            psend[i] = nn(att[...], w[:, cols_of(2 * turn(i) + 1 - c)]).astype(BF)
            p_copy(i).start()
            return carry

        lax.fori_loop(0, NY, one, 0)

    def for_me():
        def one(i, carry):
            rbuf[i] = nn(att[...], w[:, cols_of(2 * turn(i) + c)]).astype(BF)
            return carry

        lax.fori_loop(0, NY, one, 0)

    def merge():
        for i in range(NY):
            sent[p_base + i].wait_recv()
            rbuf[i] = add(rbuf[i], precv[i])

    held = {"near": [], "yo": [], "seven": []}

    def beside(arrived, slot, part, into):
        arrived.wait_recv()
        held[into].append(send(gb.at[slot, part], gb.at[slot + (2 if slot < 6 else 1), part], sib))

    def ahead():
        for i in range(2):
            beside(first[i][0], 2, quarters[i], "near")
            beside(first[i][1], 3, quarters[i + 2], "near")

    def pass_on():
        for i in range(2):
            held["yo"].append((send(gb.at[2, quarters[i]], gb.at[6, quarters[i]], yp),
                               send(gb.at[3, quarters[i + 2]], gb.at[6, quarters[i + 2]], ym)))

    def near():
        for i in range(2):
            beside(later[i][0], 2, quarters[i + 2], "near")
            beside(later[i][1], 3, quarters[i], "near")

    def second():
        for copy in held["near"]:
            copy.wait_recv()
        terms(4, 6, second_group)

    def far():
        for i in range(2):
            beside(held["yo"][i][0], 6, quarters[i], "seven")
            beside(held["yo"][i][1], 6, quarters[i + 2], "seven")

    def third():
        for copy in held["seven"]:
            copy.wait_recv()
        terms(7, 8, third_group)

    def y_far():
        held["r_far"] = [send(rbuf.at[0, top], yrp.at[1, top], yp),
                         send(rbuf.at[0, bot], yrm.at[1, bot], ym)]

    def y_early():
        held["r"] = [send(rbuf.at[1, bot], yrp.at[0, bot], yp),
                     send(rbuf.at[3, top], yrm.at[0, top], ym)]

    def y_late():
        held["r_far"][0].wait_recv()
        rbuf[1, top] = add(rbuf[1, top], yrp[1, top])
        held["r"].append(send(rbuf.at[1, top], yrp.at[0, top], yp))
        held["r_far"][1].wait_recv()
        rbuf[3, bot] = add(rbuf[3, bot], yrm[1, bot])
        held["r"].append(send(rbuf.at[3, bot], yrm.at[0, bot], ym))

    def y_end():
        for copy in held["r"]:
            copy.wait_recv()
        mixed[...] = (rbuf[2].astype(F32) + yrp[0].astype(F32) + yrm[0].astype(F32)).astype(BF)
        out_mixed.start()

    def back():
        agw[...] = acc[...].astype(BF)
        tail = agw.at[pl.ds(5 * UNIT, UNIT)]
        held["back"] = [send(tail, back_recv.at[i], to) for i, to in enumerate((prv, nxt, acr))]

    def home():
        for copy in held["back"]:
            copy.wait_recv()
        got = from_prv | from_nxt | from_acr
        ghome[pl.ds(0, 5 * UNIT), :] = agw[pl.ds(0, 5 * UNIT), :]
        for u in (5, 6, 7):
            value = jnp.zeros((UNIT, INN), F32)
            for i, slot in enumerate((6, 7, 5)):
                hit = moved(dp, slot) & (starts[slot] == u * UNIT)
                value = jnp.where(hit, back_recv[i].astype(F32), value)
            if u == 5:
                value = jnp.where(got, value, unit(agw, 5))
            ghome[pl.ds(u * UNIT, UNIT), :] = value.astype(BF)

    def backward(h, carry):
        at = pl.multiple_of(h * HEAD, HEAD)
        q_t = qkv[0, :, pl.ds(at, HEAD)].astype(F32).T.astype(BF)
        g_t = ghome[:, pl.ds(at, HEAD)].astype(F32).T.astype(BF)
        dk_t[...] = jnp.zeros_like(dk_t)
        dv_t[...] = jnp.zeros_like(dv_t)
        for i, (lo, hi) in enumerate(WINDOWS):
            rows, keys = pl.ds(i * 128, 128), pl.ds(lo, hi - lo)
            k = qkv[1, keys, pl.ds(at, HEAD)]
            v = qkv[2, keys, pl.ds(at, HEAD)]
            p = probs[h, rows, keys]
            dp_ = nt(ghome[rows, pl.ds(at, HEAD)], v)
            mean = jnp.sum(p * dp_, axis=-1, keepdims=True)
            ds = (p * (dp_ - mean) * DOWN).astype(BF)
            dqkv[0, rows, pl.ds(at, HEAD)] = nn(ds, k).astype(BF)
            mine = slice(i * 128, (i + 1) * 128)
            dk_t[:, keys] += nn(q_t[:, mine], ds)
            dv_t[:, keys] += nn(g_t[:, mine], p.astype(BF))
        dqkv[1, :, pl.ds(at, HEAD)] = dk_t[...].T.astype(BF)
        dqkv[2, :, pl.ds(at, HEAD)] = dv_t[...].T.astype(BF)
        return carry

    def heads(lo, hi):
        lax.fori_loop(lo, hi, backward, 0)
        if hi == HEADS:
            out_dqkv.start()

    lanes = slice(None)
    x2a = along_x(2, 1, second_group)
    x2b = along_x(4, 1, second_group)
    x3 = along_x(6, 1, third_group)
    z2 = [along_z(wt2, i * ZROWS, ZROWS, z2p, z2m, zr2, lanes) for i in range(COLS // ZROWS)]
    z1 = [along_z(xr, i * XROWS, XROWS, z1p, z1m, wg, pl.ds(0, LX)) for i in range(PART // XROWS)]
    xl = [along_x_last()]

    def go(rings):
        for ring in rings:
            next(ring)

    todo = {
        "P": for_sibling, "Q": for_me, "M": merge, "S": ahead, "F": pass_on, "N": near, "T2A": lambda: terms(2, 4, second_group), "T2B": second, "W": far,
        "T3A": lambda: terms(6, 7, third_group), "T3B": third, "G2": lambda: grads(2, 6, second_group), "G3": lambda: grads(6, 8, third_group),
        "YF": y_far, "YE": y_early, "YL": y_late, "YD": y_end, "BK": back, "HM": home,
        "B0": lambda: heads(0, 1), "B1": lambda: heads(1, 2), "B2": lambda: heads(2, 3),
        "B12": lambda: heads(1, 3), "B": lambda: heads(0, 3),
        "X1": lambda: next(x1), "A": lambda: next(x2a), "C": lambda: next(x2b), "X3": lambda: next(x3),
        "Z2": lambda: go(z2), "Z1": lambda: go(z1), "XL": lambda: go(xl),
    }
    for name in ORDER:
        todo[name]()
    out_wg.start()
    for copy in sent:
        copy.wait_send()
    for copy in (out_mixed, out_dqkv, out_wg):
        copy.wait()


def scratch():
    v = pltpu.VMEM
    return [
        v((3, HOME, INN), BF), v((INN, 8 * COLS), BF), v((8, CAP, COLS), BF), v((HOME, HOME), F32),
        v((HEADS, HOME, HOME), F32), v((HOME, INN), BF), v((3, UNIT, INN), BF), v((3, UNIT, INN), BF),
        v((CAP, INN), BF), v((CAP, INN), F32), v((CAP, INN), BF), v((3, UNIT, INN), BF),
        v((HOME, INN), BF), v((HEAD, HOME), F32), v((HEAD, HOME), F32),
        v((8, COLS, LX), BF), v((8, COLS, LZ), BF),
        v((4, CAP, COLS), BF), v((4, CAP, COLS), BF), v((4, CAP, COLS), BF),
        v((2, CAP, COLS), BF), v((2, CAP, COLS), BF),
        v((4, PART, LX), BF), v((4, PART, LX), BF), v((8, PART, LX), BF), v((8, PART, LX), BF),
        v((8, PART, LX), BF),
        v((4, PART, LX), BF), v((4, PART, LX), BF), v((4, COLS, LZ), BF), v((4, COLS, LZ), BF),
        v((COLS, LZ), BF), v((2, PART, LZ), BF), v((2, PART, LZ), BF),
        v((CAP, COLS), BF), v((3, HOME, INN), BF), v((PART, INN), BF),
        pltpu.SemaphoreType.DMA((112,)), pltpu.SemaphoreType.DMA((112,)), pltpu.SemaphoreType.DMA((6,)),
    ]


def body(qkv_rows, out_weight, out_grad, image_len, dest_rank, dest_offset):
    smem = pl.BlockSpec(memory_space=pltpu.SMEM)
    anywhere = pl.BlockSpec(memory_space=pl.ANY)
    mixed, dqkv, turned = pl.pallas_call(
        kernel,
        out_shape=(
            jax.ShapeDtypeStruct((CAP, COLS), BF),
            jax.ShapeDtypeStruct((3, HOME, INN), BF),
            jax.ShapeDtypeStruct((192, INN), BF),
        ),
        in_specs=[smem, smem, anywhere, anywhere, anywhere],
        out_specs=(anywhere, anywhere, anywhere),
        scratch_shapes=scratch(),
        compiler_params=pltpu.CompilerParams(
            collective_id=0, has_side_effects=True, vmem_limit_bytes=60 * 2**20),
    )(image_len, dest_rank, jnp.transpose(qkv_rows, (1, 0, 2)), out_weight, out_grad)
    return mixed, jnp.transpose(dqkv, (1, 0, 2)), turned.T


def solution(mesh):
    return jax.shard_map(
        body,
        mesh=mesh,
        in_specs=(P("dp", None, "mp"), P("mp", None), P("dp", "mp"), P(), P(), P()),
        out_specs=(P("dp", "mp"), P("dp", None, "mp"), P("mp", "dp")),
        check_vma=False,
    )
```

```python
import functools

import jax
import jax.numpy as jnp
from jax import lax
from jax.experimental import pallas as pl
from jax.experimental.pallas import tpu as pltpu
from jax.sharding import PartitionSpec as P

HEAD = 128
UNIT = 64
SLOTS = 8
NZ, NX, NY = 8, 4, 4
NDP = NZ * NX
HOME = 512
CAP = 384
HEADS = 3
INN = HEADS * HEAD
COLS = 768
DOWN = 1 / HEAD ** 0.5
MESH = pl.DeviceIdType.MESH
F32 = jnp.float32
BF = jnp.bfloat16
HALF = CAP // 2
LX = 256
LZ = INN - LX
PART = COLS // NX
ZROWS = 384
XROWS = 96
QUARTER = CAP // 4
WINDOWS = ((0, 384), (0, 512), (0, 512), (128, 512))


ORDER = (
    "P", "S", "F", "Q", "X1", "N", "T2A", "A", "T2B", "C", "M", "A", "G2", "X1", "W", "YF", "YE", "T3A",
    "T3B", "Z2", "X3", "C", "A", "G3", "BK", "Z2", "C", "YL", "X3", "HM", "Z2", "X3", "Z1", "B0", "Z2",
    "Z1", "B1", "Z2", "XL", "Z1", "YD", "XL", "Z1", "XL", "B2", "Z1",
)


def add(a, b):
    return (a.astype(F32) + b.astype(F32)).astype(BF)


def nt(a, b):
    return lax.dot_general(a, b, (((1,), (1,)), ((), ())), preferred_element_type=F32)


def nn(a, b):
    return jnp.dot(a, b, preferred_element_type=F32)


def kernel(len_ref, dest_ref, qkv_hbm, w_hbm, g_hbm, mixed_hbm, dqkv_hbm, wg_hbm,
           qkv, w, gb, bias, probs, att_home, att_send, att_recv, att, acc, agw, back_recv,
           ghome, dk_t, dv_t, wt1, wt2, psend, precv, rbuf, yrp, yrm, xlp, xlm, xrp, xrm, xr,
           z1p, z1m, z2p, z2m, zr2, x2p, x2m, mixed, dqkv, wg, ss, rs, ls):
    dp, mp = lax.axis_index("dp"), lax.axis_index("mp")
    z, x = lax.div(dp, NX), lax.rem(dp, NX)
    y, c = lax.div(mp, 2), lax.rem(mp, 2)

    def at_y(d):
        return lax.rem(y + d + NY, NY)

    def at_x(d):
        return lax.rem(x + d + NX, NX)

    def at_z(d):
        return lax.rem(z + d + NZ, NZ)

    def at_dp(d):
        return lax.rem(dp + d + NDP, NDP)

    sib = (dp, 2 * y + 1 - c)
    yp, ym = (dp, 2 * at_y(1) + c), (dp, 2 * at_y(-1) + c)
    xp, xm = (z * NX + at_x(1), mp), (z * NX + at_x(-1), mp)
    zp, zm = (at_z(1) * NX + x, mp), (at_z(-1) * NX + x, mp)
    nxt, prv, acr = (at_dp(1), mp), (at_dp(-1), mp), (at_dp(NDP // 2), mp)
    partners = (sib, yp, ym, xp, xm, zp, zm, nxt, prv, acr)

    in_g = pltpu.make_async_copy(g_hbm, gb.at[0], ls.at[0])
    in_qkv = pltpu.make_async_copy(qkv_hbm, qkv, ls.at[1])
    in_w = pltpu.make_async_copy(w_hbm, w, ls.at[2])
    out_mixed = pltpu.make_async_copy(mixed, mixed_hbm, ls.at[3])
    out_dqkv = pltpu.make_async_copy(dqkv, dqkv_hbm, ls.at[4])
    out_wg = pltpu.make_async_copy(wg, wg_hbm, ls.at[5])
    in_g.start()
    in_qkv.start()
    in_w.start()

    barrier = pltpu.get_barrier_semaphore()
    for one in partners:
        pl.semaphore_signal(barrier, inc=1, device_id=one, device_id_type=MESH)
    pl.semaphore_wait(barrier, len(partners))

    sent = []

    def send(src, dst, to):
        i = len(sent)
        copy = pltpu.make_async_remote_copy(
            src_ref=src, dst_ref=dst, send_sem=ss.at[i], recv_sem=rs.at[i], device_id=to,
            device_id_type=MESH)
        copy.start()
        sent.append(copy)
        return copy

    top, bot = pl.ds(0, HALF), pl.ds(HALF, HALF)

    in_g.wait()
    quarters = [pl.ds(i * QUARTER, QUARTER) for i in range(4)]
    first, later = {}, {}
    for i in range(2):
        first[i] = (send(gb.at[0, quarters[i]], gb.at[2, quarters[i]], yp),
                    send(gb.at[0, quarters[i + 2]], gb.at[3, quarters[i + 2]], ym))
    g_sib = send(gb.at[0], gb.at[1], sib)

    def ends_of(rank):
        ends, total = [], jnp.int32(0)
        for s in range(SLOTS):
            total = total + len_ref[rank * SLOTS + s]
            ends.append(total)
        return ends

    ends = ends_of(dp)

    def moved(rank, slot):
        return (dest_ref[rank * SLOTS + slot] != rank) & (len_ref[rank * SLOTS + slot] > 0)

    def image_of(pos):
        out = jnp.zeros(pos.shape, jnp.int32)
        for end in ends:
            out = out + (pos >= end).astype(jnp.int32)
        return out

    rows_at = image_of(lax.broadcasted_iota(jnp.int32, (HOME, 1), 0))
    cols_at = image_of(lax.broadcasted_iota(jnp.int32, (1, HOME), 1))
    bias[...] = jnp.where(rows_at == cols_at, 0.0, -1e30).astype(F32)

    in_qkv.wait()

    def forward(h, carry):
        at = pl.multiple_of(h * HEAD, HEAD)
        for i, (lo, hi) in enumerate(WINDOWS):
            rows, keys = pl.ds(i * 128, 128), pl.ds(lo, hi - lo)
            q = qkv[0, rows, pl.ds(at, HEAD)]
            k = qkv[1, keys, pl.ds(at, HEAD)]
            v = qkv[2, keys, pl.ds(at, HEAD)]
            s = nt(q, k) * DOWN + bias[rows, keys]
            e = jnp.exp(s - jnp.max(s, axis=-1, keepdims=True))
            p = e / jnp.sum(e, axis=-1, keepdims=True)
            probs[h, rows, keys] = p
            att_home[rows, pl.ds(at, HEAD)] = nn(p.astype(BF), v).astype(BF)
        return carry

    lax.fori_loop(0, HEADS, forward, 0)
    for i in range(2):
        later[i] = (send(gb.at[0, quarters[i + 2]], gb.at[2, quarters[i + 2]], yp),
                    send(gb.at[0, quarters[i]], gb.at[3, quarters[i]], ym))

    def unit(ref, u):
        return ref[pl.ds(u * UNIT, UNIT), :].astype(F32)

    starts = [jnp.int32(0)] + ends[:-1]
    for i, slot in enumerate((6, 7, 5)):
        pick = jnp.where(starts[slot] == 5 * UNIT, unit(att_home, 5),
                         jnp.where(starts[slot] == 6 * UNIT, unit(att_home, 6), unit(att_home, 7)))
        att_send[i] = pick.astype(BF)
    moves = [send(att_send.at[i], att_recv.at[i], to) for i, to in enumerate((nxt, prv, acr))]

    def flip_of(f):
        return c + f - 2 * c * f

    def first_group(j):
        return 2 * y + flip_of(j)

    def second_group(j):
        i = j - 2
        return 2 * at_y(2 * lax.rem(i, 2) - 1) + flip_of(lax.div(i, 2))

    def third_group(j):
        return 2 * at_y(2) + flip_of(j - 6)

    def cols_of(block):
        return pl.ds(pl.multiple_of(block * COLS, COLS), COLS)

    def terms(lo, hi, block_of):
        def one(j, carry):
            t = lax.dot_general(gb[j], att[...], (((0,), (0,)), ((), ())),
                                preferred_element_type=F32).astype(BF)
            wt1[j] = t[:, :LX]
            wt2[block_of(j)] = t[:, LX:]
            return carry

        lax.fori_loop(lo, hi, one, 0)

    def grads(lo, hi, block_of):
        def one(j, carry):
            acc[...] += nt(gb[j], w[:, cols_of(block_of(j))])
            return carry

        lax.fori_loop(lo, hi, one, 0)

    def along_x(lo, half, block_of):
        far, right, left = (pl.ds(pl.multiple_of(at_x(d) * PART, PART), PART) for d in (2, 1, -1))
        mine = pl.ds(pl.multiple_of(x * PART, PART), PART)
        a, b = pl.ds(lo, half), pl.ds(lo + half, half)
        la = pl.ds(lo // 2, half)
        relay_p = send(wt1.at[a, far], xlp.at[la], xp)
        relay_m = send(wt1.at[b, far], xlm.at[la], xm)
        early_p = send(wt1.at[b, right], xrp.at[b], xp)
        early_m = send(wt1.at[a, left], xrm.at[a], xm)
        yield
        relay_p.wait_recv()
        for i in range(half):
            wt1[lo + i, right] = add(wt1[lo + i, right], xlp[lo // 2 + i])
        late_p = send(wt1.at[a, right], xrp.at[a], xp)
        relay_m.wait_recv()
        for i in range(half):
            wt1[lo + half + i, left] = add(wt1[lo + half + i, left], xlm[lo // 2 + i])
        late_m = send(wt1.at[b, left], xrm.at[b], xm)
        yield
        for copy in (early_p, early_m, late_p, late_m):
            copy.wait_recv()

        def one(j, carry):
            total = wt1[j, mine].astype(F32) + xrp[j].astype(F32) + xrm[j].astype(F32)
            xr[block_of(j)] = total.astype(BF)
            return carry

        lax.fori_loop(lo, lo + 2 * half, one, 0)
        yield

    def along_z(buf, first, rows, from_m, from_p, out, lanes):
        half = rows // 2
        up, down, both = pl.ds(first, half), pl.ds(first + half, half), pl.ds(first, rows)
        a = send(buf.at[at_z(4), up], from_m.at[3, up], zp)
        b = send(buf.at[at_z(4), down], from_p.at[3, down], zm)
        yield
        for d in (3, 2, 1):
            part_a, part_b = (up, down) if d == 3 else (both, both)
            a.wait_recv()
            here = at_z(d)
            buf[here, part_a] = add(buf[here, part_a], from_m[d, part_a])
            a = send(buf.at[here, both], from_m.at[d - 1, both], zp)
            b.wait_recv()
            here = at_z(-d)
            buf[here, part_b] = add(buf[here, part_b], from_p[d, part_b])
            b = send(buf.at[here, both], from_p.at[d - 1, both], zm)
            yield
        a.wait_recv()
        b.wait_recv()
        total = buf[z, both].astype(F32) + from_m[0, both].astype(F32) + from_p[0, both].astype(F32)
        out[both, lanes] = total.astype(BF)
        yield

    def along_x_last():
        far, right, left, mine = (pl.multiple_of(at_x(d) * PART, PART) for d in (2, 1, -1, 0))
        half = PART // 2
        up, down = pl.ds(0, half), pl.ds(half, half)
        a = send(zr2.at[pl.ds(far, half)], x2p.at[1, up], xp)
        b = send(zr2.at[pl.ds(pl.multiple_of(far + half, half), half)], x2m.at[1, down], xm)
        yield
        a.wait_recv()
        zr2[pl.ds(right, half)] = add(zr2[pl.ds(right, half)], x2p[1, up])
        a = send(zr2.at[pl.ds(right, PART)], x2p.at[0], xp)
        b.wait_recv()
        low = pl.ds(pl.multiple_of(left + half, half), half)
        zr2[low] = add(zr2[low], x2m[1, down])
        b = send(zr2.at[pl.ds(left, PART)], x2m.at[0], xm)
        yield
        a.wait_recv()
        b.wait_recv()
        total = zr2[pl.ds(mine, PART)].astype(F32) + x2p[0].astype(F32) + x2m[0].astype(F32)
        wg[:, LX:] = total.astype(BF)
        yield

    in_w.wait()
    acc[...] = jnp.zeros_like(acc)
    g_sib.wait_recv()
    grads(0, 2, first_group)

    for m in moves:
        m.wait_recv()
    from_prv, from_nxt, from_acr = moved(at_dp(-1), 6), moved(at_dp(1), 7), moved(at_dp(NDP // 2), 5)
    last = jnp.where(from_prv, att_recv[0].astype(F32),
                     jnp.where(from_nxt, att_recv[1].astype(F32),
                               jnp.where(from_acr, att_recv[2].astype(F32), unit(att_home, 5))))
    att[pl.ds(0, 5 * UNIT), :] = att_home[pl.ds(0, 5 * UNIT), :]
    att[pl.ds(5 * UNIT, UNIT), :] = last.astype(BF)

    terms(0, 2, first_group)
    x1 = along_x(0, 1, first_group)
    next(x1)

    def turn(i):
        return lax.rem(y + 2 + 3 * i, NY)

    p_base = len(sent)

    def p_copy(i):
        return pltpu.make_async_remote_copy(
            src_ref=psend.at[i], dst_ref=precv.at[i], send_sem=ss.at[p_base + i],
            recv_sem=rs.at[p_base + i], device_id=sib, device_id_type=MESH)

    sent.extend(p_copy(i) for i in range(NY))

    def for_sibling():
        def one(i, carry):
            psend[i] = nn(att[...], w[:, cols_of(2 * turn(i) + 1 - c)]).astype(BF)
            p_copy(i).start()
            return carry

        lax.fori_loop(0, NY, one, 0)

    def for_me():
        def one(i, carry):
            rbuf[i] = nn(att[...], w[:, cols_of(2 * turn(i) + c)]).astype(BF)
            return carry

        lax.fori_loop(0, NY, one, 0)

    def merge():
        for i in range(NY):
            sent[p_base + i].wait_recv()
            rbuf[i] = add(rbuf[i], precv[i])

    held = {"near": [], "yo": [], "seven": []}

    def beside(arrived, slot, part, into):
        arrived.wait_recv()
        held[into].append(send(gb.at[slot, part], gb.at[slot + (2 if slot < 6 else 1), part], sib))

    def ahead():
        for i in range(2):
            beside(first[i][0], 2, quarters[i], "near")
            beside(first[i][1], 3, quarters[i + 2], "near")

    def pass_on():
        for i in range(2):
            held["yo"].append((send(gb.at[2, quarters[i]], gb.at[6, quarters[i]], yp),
                               send(gb.at[3, quarters[i + 2]], gb.at[6, quarters[i + 2]], ym)))

    def near():
        for i in range(2):
            beside(later[i][0], 2, quarters[i + 2], "near")
            beside(later[i][1], 3, quarters[i], "near")

    def second():
        for copy in held["near"]:
            copy.wait_recv()
        terms(4, 6, second_group)

    def far():
        for i in range(2):
            beside(held["yo"][i][0], 6, quarters[i], "seven")
            beside(held["yo"][i][1], 6, quarters[i + 2], "seven")

    def third():
        for copy in held["seven"]:
            copy.wait_recv()
        terms(7, 8, third_group)

    def y_far():
        held["r_far"] = [send(rbuf.at[0, top], yrp.at[1, top], yp),
                         send(rbuf.at[0, bot], yrm.at[1, bot], ym)]

    def y_early():
        held["r"] = [send(rbuf.at[1, bot], yrp.at[0, bot], yp),
                     send(rbuf.at[3, top], yrm.at[0, top], ym)]

    def y_late():
        held["r_far"][0].wait_recv()
        rbuf[1, top] = add(rbuf[1, top], yrp[1, top])
        held["r"].append(send(rbuf.at[1, top], yrp.at[0, top], yp))
        held["r_far"][1].wait_recv()
        rbuf[3, bot] = add(rbuf[3, bot], yrm[1, bot])
        held["r"].append(send(rbuf.at[3, bot], yrm.at[0, bot], ym))

    def y_end():
        for copy in held["r"]:
            copy.wait_recv()
        mixed[...] = (rbuf[2].astype(F32) + yrp[0].astype(F32) + yrm[0].astype(F32)).astype(BF)
        out_mixed.start()

    def back():
        agw[...] = acc[...].astype(BF)
        tail = agw.at[pl.ds(5 * UNIT, UNIT)]
        held["back"] = [send(tail, back_recv.at[i], to) for i, to in enumerate((prv, nxt, acr))]

    def home():
        for copy in held["back"]:
            copy.wait_recv()
        got = from_prv | from_nxt | from_acr
        ghome[pl.ds(0, 5 * UNIT), :] = agw[pl.ds(0, 5 * UNIT), :]
        for u in (5, 6, 7):
            value = jnp.zeros((UNIT, INN), F32)
            for i, slot in enumerate((6, 7, 5)):
                hit = moved(dp, slot) & (starts[slot] == u * UNIT)
                value = jnp.where(hit, back_recv[i].astype(F32), value)
            if u == 5:
                value = jnp.where(got, value, unit(agw, 5))
            ghome[pl.ds(u * UNIT, UNIT), :] = value.astype(BF)

    def backward(h, carry):
        at = pl.multiple_of(h * HEAD, HEAD)
        q_t = qkv[0, :, pl.ds(at, HEAD)].astype(F32).T.astype(BF)
        g_t = ghome[:, pl.ds(at, HEAD)].astype(F32).T.astype(BF)
        dk_t[...] = jnp.zeros_like(dk_t)
        dv_t[...] = jnp.zeros_like(dv_t)
        for i, (lo, hi) in enumerate(WINDOWS):
            rows, keys = pl.ds(i * 128, 128), pl.ds(lo, hi - lo)
            k = qkv[1, keys, pl.ds(at, HEAD)]
            v = qkv[2, keys, pl.ds(at, HEAD)]
            p = probs[h, rows, keys]
            dp_ = nt(ghome[rows, pl.ds(at, HEAD)], v)
            mean = jnp.sum(p * dp_, axis=-1, keepdims=True)
            ds = (p * (dp_ - mean) * DOWN).astype(BF)
            dqkv[0, rows, pl.ds(at, HEAD)] = nn(ds, k).astype(BF)
            mine = slice(i * 128, (i + 1) * 128)
            dk_t[:, keys] += nn(q_t[:, mine], ds)
            dv_t[:, keys] += nn(g_t[:, mine], p.astype(BF))
        dqkv[1, :, pl.ds(at, HEAD)] = dk_t[...].T.astype(BF)
        dqkv[2, :, pl.ds(at, HEAD)] = dv_t[...].T.astype(BF)
        return carry

    def heads(lo, hi):
        lax.fori_loop(lo, hi, backward, 0)
        if hi == HEADS:
            out_dqkv.start()

    lanes = slice(None)
    x2a = along_x(2, 1, second_group)
    x2b = along_x(4, 1, second_group)
    x3 = along_x(6, 1, third_group)
    z2 = [along_z(wt2, i * ZROWS, ZROWS, z2p, z2m, zr2, lanes) for i in range(COLS // ZROWS)]
    z1 = [along_z(xr, i * XROWS, XROWS, z1p, z1m, wg, pl.ds(0, LX)) for i in range(PART // XROWS)]
    xl = [along_x_last()]

    def go(rings):
        for ring in rings:
            next(ring)

    todo = {
        "P": for_sibling, "Q": for_me, "M": merge, "S": ahead, "F": pass_on, "N": near, "T2A": lambda: terms(2, 4, second_group), "T2B": second, "W": far,
        "T3A": lambda: terms(6, 7, third_group), "T3B": third, "G2": lambda: grads(2, 6, second_group), "G3": lambda: grads(6, 8, third_group),
        "YF": y_far, "YE": y_early, "YL": y_late, "YD": y_end, "BK": back, "HM": home,
        "B0": lambda: heads(0, 1), "B1": lambda: heads(1, 2), "B2": lambda: heads(2, 3),
        "B12": lambda: heads(1, 3), "B": lambda: heads(0, 3),
        "X1": lambda: next(x1), "A": lambda: next(x2a), "C": lambda: next(x2b), "X3": lambda: next(x3),
        "Z2": lambda: go(z2), "Z1": lambda: go(z1), "XL": lambda: go(xl),
    }
    for name in ORDER:
        todo[name]()
    out_wg.start()
    for copy in sent:
        copy.wait_send()
    for copy in (out_mixed, out_dqkv, out_wg):
        copy.wait()


def scratch():
    v = pltpu.VMEM
    return [
        v((3, HOME, INN), BF), v((INN, 8 * COLS), BF), v((8, CAP, COLS), BF), v((HOME, HOME), F32),
        v((HEADS, HOME, HOME), F32), v((HOME, INN), BF), v((3, UNIT, INN), BF), v((3, UNIT, INN), BF),
        v((CAP, INN), BF), v((CAP, INN), F32), v((CAP, INN), BF), v((3, UNIT, INN), BF),
        v((HOME, INN), BF), v((HEAD, HOME), F32), v((HEAD, HOME), F32),
        v((8, COLS, LX), BF), v((8, COLS, LZ), BF),
        v((4, CAP, COLS), BF), v((4, CAP, COLS), BF), v((4, CAP, COLS), BF),
        v((2, CAP, COLS), BF), v((2, CAP, COLS), BF),
        v((4, PART, LX), BF), v((4, PART, LX), BF), v((8, PART, LX), BF), v((8, PART, LX), BF),
        v((8, PART, LX), BF),
        v((4, PART, LX), BF), v((4, PART, LX), BF), v((4, COLS, LZ), BF), v((4, COLS, LZ), BF),
        v((COLS, LZ), BF), v((2, PART, LZ), BF), v((2, PART, LZ), BF),
        v((CAP, COLS), BF), v((3, HOME, INN), BF), v((PART, INN), BF),
        pltpu.SemaphoreType.DMA((112,)), pltpu.SemaphoreType.DMA((112,)), pltpu.SemaphoreType.DMA((6,)),
    ]


def body(qkv_rows, out_weight, out_grad, image_len, dest_rank, dest_offset):
    smem = pl.BlockSpec(memory_space=pltpu.SMEM)
    anywhere = pl.BlockSpec(memory_space=pl.ANY)
    mixed, dqkv, turned = pl.pallas_call(
        kernel,
        out_shape=(
            jax.ShapeDtypeStruct((CAP, COLS), BF),
            jax.ShapeDtypeStruct((3, HOME, INN), BF),
            jax.ShapeDtypeStruct((192, INN), BF),
        ),
        in_specs=[smem, smem, anywhere, anywhere, anywhere],
        out_specs=(anywhere, anywhere, anywhere),
        scratch_shapes=scratch(),
        compiler_params=pltpu.CompilerParams(
            collective_id=0, has_side_effects=True, vmem_limit_bytes=60 * 2**20),
    )(image_len, dest_rank, jnp.transpose(qkv_rows, (1, 0, 2)), out_weight, out_grad)
    return mixed, jnp.transpose(dqkv, (1, 0, 2)), turned.T


def solution(mesh):
    return jax.shard_map(
        body,
        mesh=mesh,
        in_specs=(P("dp", None, "mp"), P("mp", None), P("dp", "mp"), P(), P(), P()),
        out_specs=(P("dp", "mp"), P("dp", None, "mp"), P("mp", "dp")),
        check_vma=False,
    )
```

```python
import functools

import jax
import jax.numpy as jnp
from jax import lax
from jax.experimental import pallas as pl
from jax.experimental.pallas import tpu as pltpu
from jax.sharding import PartitionSpec as P

HEAD = 128
UNIT = 64
SLOTS = 8
NZ, NX, NY = 8, 4, 4
NDP = NZ * NX
HOME = 512
CAP = 384
HEADS = 3
INN = HEADS * HEAD
COLS = 768
DOWN = 1 / HEAD ** 0.5
MESH = pl.DeviceIdType.MESH
F32 = jnp.float32
BF = jnp.bfloat16
HALF = CAP // 2
LX = 256
LZ = INN - LX
PART = COLS // NX
ZROWS = 384
XROWS = 96
QUARTER = CAP // 4
WINDOWS = ((0, 384), (0, 512), (0, 512), (128, 512))


ORDER = (
    "P", "S", "F", "Q", "X1", "N", "T2A", "A", "T2B", "C", "M", "A", "G2", "X1", "W", "YF", "YE", "T3A",
    "T3B", "Z2", "X3", "C", "A", "G3", "BK", "Z2", "C", "YL", "X3", "HM", "Z2", "X3", "Z1", "B0", "Z2",
    "Z1", "B1", "Z2", "XL", "Z1", "YD", "XL", "Z1", "XL", "B2", "Z1",
)


def add(a, b):
    return (a.astype(F32) + b.astype(F32)).astype(BF)


def nt(a, b):
    return lax.dot_general(a, b, (((1,), (1,)), ((), ())), preferred_element_type=F32)


def nn(a, b):
    return jnp.dot(a, b, preferred_element_type=F32)


def kernel(len_ref, dest_ref, qkv_hbm, w_hbm, g_hbm, mixed_hbm, dqkv_hbm, wg_hbm,
           qkv, w, gb, bias, probs, att_home, att_send, att_recv, att, acc, agw, back_recv,
           ghome, dk_t, dv_t, wt1, wt2, psend, precv, rbuf, yrp, yrm, xlp, xlm, xrp, xrm, xr,
           z1p, z1m, z2p, z2m, zr2, x2p, x2m, mixed, dqkv, wg, ss, rs, ls):
    dp, mp = lax.axis_index("dp"), lax.axis_index("mp")
    z, x = lax.div(dp, NX), lax.rem(dp, NX)
    y, c = lax.div(mp, 2), lax.rem(mp, 2)

    def at_y(d):
        return lax.rem(y + d + NY, NY)

    def at_x(d):
        return lax.rem(x + d + NX, NX)

    def at_z(d):
        return lax.rem(z + d + NZ, NZ)

    def at_dp(d):
        return lax.rem(dp + d + NDP, NDP)

    sib = (dp, 2 * y + 1 - c)
    yp, ym = (dp, 2 * at_y(1) + c), (dp, 2 * at_y(-1) + c)
    xp, xm = (z * NX + at_x(1), mp), (z * NX + at_x(-1), mp)
    zp, zm = (at_z(1) * NX + x, mp), (at_z(-1) * NX + x, mp)
    nxt, prv, acr = (at_dp(1), mp), (at_dp(-1), mp), (at_dp(NDP // 2), mp)
    partners = (sib, yp, ym, xp, xm, zp, zm, nxt, prv, acr)

    in_g = pltpu.make_async_copy(g_hbm, gb.at[0], ls.at[0])
    in_qkv = pltpu.make_async_copy(qkv_hbm, qkv, ls.at[1])
    in_w = pltpu.make_async_copy(w_hbm, w, ls.at[2])
    out_mixed = pltpu.make_async_copy(mixed, mixed_hbm, ls.at[3])
    out_dqkv = pltpu.make_async_copy(dqkv, dqkv_hbm, ls.at[4])
    out_wg = pltpu.make_async_copy(wg, wg_hbm, ls.at[5])
    in_g.start()
    in_qkv.start()
    in_w.start()

    barrier = pltpu.get_barrier_semaphore()
    for one in partners:
        pl.semaphore_signal(barrier, inc=1, device_id=one, device_id_type=MESH)
    pl.semaphore_wait(barrier, len(partners))

    sent = []

    def send(src, dst, to):
        i = len(sent)
        copy = pltpu.make_async_remote_copy(
            src_ref=src, dst_ref=dst, send_sem=ss.at[i], recv_sem=rs.at[i], device_id=to,
            device_id_type=MESH)
        copy.start()
        sent.append(copy)
        return copy

    top, bot = pl.ds(0, HALF), pl.ds(HALF, HALF)

    in_g.wait()
    quarters = [pl.ds(i * QUARTER, QUARTER) for i in range(4)]
    first, later = {}, {}
    for i in range(2):
        first[i] = (send(gb.at[0, quarters[i]], gb.at[2, quarters[i]], yp),
                    send(gb.at[0, quarters[i + 2]], gb.at[3, quarters[i + 2]], ym))
    for i in range(2):
        later[i] = (send(gb.at[0, quarters[i + 2]], gb.at[2, quarters[i + 2]], yp),
                    send(gb.at[0, quarters[i]], gb.at[3, quarters[i]], ym))
    g_sib = send(gb.at[0], gb.at[1], sib)

    def ends_of(rank):
        ends, total = [], jnp.int32(0)
        for s in range(SLOTS):
            total = total + len_ref[rank * SLOTS + s]
            ends.append(total)
        return ends

    ends = ends_of(dp)

    def moved(rank, slot):
        return (dest_ref[rank * SLOTS + slot] != rank) & (len_ref[rank * SLOTS + slot] > 0)

    def image_of(pos):
        out = jnp.zeros(pos.shape, jnp.int32)
        for end in ends:
            out = out + (pos >= end).astype(jnp.int32)
        return out

    rows_at = image_of(lax.broadcasted_iota(jnp.int32, (HOME, 1), 0))
    cols_at = image_of(lax.broadcasted_iota(jnp.int32, (1, HOME), 1))
    bias[...] = jnp.where(rows_at == cols_at, 0.0, -1e30).astype(F32)

    in_qkv.wait()

    def forward(h, carry):
        at = pl.multiple_of(h * HEAD, HEAD)
        for i, (lo, hi) in enumerate(WINDOWS):
            rows, keys = pl.ds(i * 128, 128), pl.ds(lo, hi - lo)
            q = qkv[0, rows, pl.ds(at, HEAD)]
            k = qkv[1, keys, pl.ds(at, HEAD)]
            v = qkv[2, keys, pl.ds(at, HEAD)]
            s = nt(q, k) * DOWN + bias[rows, keys]
            e = jnp.exp(s - jnp.max(s, axis=-1, keepdims=True))
            p = e / jnp.sum(e, axis=-1, keepdims=True)
            probs[h, rows, keys] = p
            att_home[rows, pl.ds(at, HEAD)] = nn(p.astype(BF), v).astype(BF)
        return carry

    lax.fori_loop(0, HEADS, forward, 0)

    def unit(ref, u):
        return ref[pl.ds(u * UNIT, UNIT), :].astype(F32)

    starts = [jnp.int32(0)] + ends[:-1]
    for i, slot in enumerate((6, 7, 5)):
        pick = jnp.where(starts[slot] == 5 * UNIT, unit(att_home, 5),
                         jnp.where(starts[slot] == 6 * UNIT, unit(att_home, 6), unit(att_home, 7)))
        att_send[i] = pick.astype(BF)
    moves = [send(att_send.at[i], att_recv.at[i], to) for i, to in enumerate((nxt, prv, acr))]

    def flip_of(f):
        return c + f - 2 * c * f

    def first_group(j):
        return 2 * y + flip_of(j)

    def second_group(j):
        i = j - 2
        return 2 * at_y(2 * lax.rem(i, 2) - 1) + flip_of(lax.div(i, 2))

    def third_group(j):
        return 2 * at_y(2) + flip_of(j - 6)

    def cols_of(block):
        return pl.ds(pl.multiple_of(block * COLS, COLS), COLS)

    def terms(lo, hi, block_of):
        def one(j, carry):
            t = lax.dot_general(gb[j], att[...], (((0,), (0,)), ((), ())),
                                preferred_element_type=F32).astype(BF)
            wt1[j] = t[:, :LX]
            wt2[block_of(j)] = t[:, LX:]
            return carry

        lax.fori_loop(lo, hi, one, 0)

    def grads(lo, hi, block_of):
        def one(j, carry):
            acc[...] += nt(gb[j], w[:, cols_of(block_of(j))])
            return carry

        lax.fori_loop(lo, hi, one, 0)

    def along_x(lo, half, block_of):
        far, right, left = (pl.ds(pl.multiple_of(at_x(d) * PART, PART), PART) for d in (2, 1, -1))
        mine = pl.ds(pl.multiple_of(x * PART, PART), PART)
        a, b = pl.ds(lo, half), pl.ds(lo + half, half)
        la = pl.ds(lo // 2, half)
        relay_p = send(wt1.at[a, far], xlp.at[la], xp)
        relay_m = send(wt1.at[b, far], xlm.at[la], xm)
        early_p = send(wt1.at[b, right], xrp.at[b], xp)
        early_m = send(wt1.at[a, left], xrm.at[a], xm)
        yield
        relay_p.wait_recv()
        for i in range(half):
            wt1[lo + i, right] = add(wt1[lo + i, right], xlp[lo // 2 + i])
        late_p = send(wt1.at[a, right], xrp.at[a], xp)
        relay_m.wait_recv()
        for i in range(half):
            wt1[lo + half + i, left] = add(wt1[lo + half + i, left], xlm[lo // 2 + i])
        late_m = send(wt1.at[b, left], xrm.at[b], xm)
        yield
        for copy in (early_p, early_m, late_p, late_m):
            copy.wait_recv()

        def one(j, carry):
            total = wt1[j, mine].astype(F32) + xrp[j].astype(F32) + xrm[j].astype(F32)
            xr[block_of(j)] = total.astype(BF)
            return carry

        lax.fori_loop(lo, lo + 2 * half, one, 0)
        yield

    def along_z(buf, first, rows, from_m, from_p, out, lanes):
        half = rows // 2
        up, down, both = pl.ds(first, half), pl.ds(first + half, half), pl.ds(first, rows)
        a = send(buf.at[at_z(4), up], from_m.at[3, up], zp)
        b = send(buf.at[at_z(4), down], from_p.at[3, down], zm)
        yield
        for d in (3, 2, 1):
            part_a, part_b = (up, down) if d == 3 else (both, both)
            a.wait_recv()
            here = at_z(d)
            buf[here, part_a] = add(buf[here, part_a], from_m[d, part_a])
            a = send(buf.at[here, both], from_m.at[d - 1, both], zp)
            b.wait_recv()
            here = at_z(-d)
            buf[here, part_b] = add(buf[here, part_b], from_p[d, part_b])
            b = send(buf.at[here, both], from_p.at[d - 1, both], zm)
            yield
        a.wait_recv()
        b.wait_recv()
        total = buf[z, both].astype(F32) + from_m[0, both].astype(F32) + from_p[0, both].astype(F32)
        out[both, lanes] = total.astype(BF)
        yield

    def along_x_last():
        far, right, left, mine = (pl.multiple_of(at_x(d) * PART, PART) for d in (2, 1, -1, 0))
        half = PART // 2
        up, down = pl.ds(0, half), pl.ds(half, half)
        a = send(zr2.at[pl.ds(far, half)], x2p.at[1, up], xp)
        b = send(zr2.at[pl.ds(pl.multiple_of(far + half, half), half)], x2m.at[1, down], xm)
        yield
        a.wait_recv()
        zr2[pl.ds(right, half)] = add(zr2[pl.ds(right, half)], x2p[1, up])
        a = send(zr2.at[pl.ds(right, PART)], x2p.at[0], xp)
        b.wait_recv()
        low = pl.ds(pl.multiple_of(left + half, half), half)
        zr2[low] = add(zr2[low], x2m[1, down])
        b = send(zr2.at[pl.ds(left, PART)], x2m.at[0], xm)
        yield
        a.wait_recv()
        b.wait_recv()
        total = zr2[pl.ds(mine, PART)].astype(F32) + x2p[0].astype(F32) + x2m[0].astype(F32)
        wg[:, LX:] = total.astype(BF)
        yield

    in_w.wait()
    acc[...] = jnp.zeros_like(acc)
    g_sib.wait_recv()
    grads(0, 2, first_group)

    for m in moves:
        m.wait_recv()
    from_prv, from_nxt, from_acr = moved(at_dp(-1), 6), moved(at_dp(1), 7), moved(at_dp(NDP // 2), 5)
    last = jnp.where(from_prv, att_recv[0].astype(F32),
                     jnp.where(from_nxt, att_recv[1].astype(F32),
                               jnp.where(from_acr, att_recv[2].astype(F32), unit(att_home, 5))))
    att[pl.ds(0, 5 * UNIT), :] = att_home[pl.ds(0, 5 * UNIT), :]
    att[pl.ds(5 * UNIT, UNIT), :] = last.astype(BF)

    terms(0, 2, first_group)
    x1 = along_x(0, 1, first_group)
    next(x1)

    def turn(i):
        return lax.rem(y + 2 + 3 * i, NY)

    p_base = len(sent)

    def p_copy(i):
        return pltpu.make_async_remote_copy(
            src_ref=psend.at[i], dst_ref=precv.at[i], send_sem=ss.at[p_base + i],
            recv_sem=rs.at[p_base + i], device_id=sib, device_id_type=MESH)

    sent.extend(p_copy(i) for i in range(NY))

    def for_sibling():
        def one(i, carry):
            psend[i] = nn(att[...], w[:, cols_of(2 * turn(i) + 1 - c)]).astype(BF)
            p_copy(i).start()
            return carry

        lax.fori_loop(0, NY, one, 0)

    def for_me():
        def one(i, carry):
            rbuf[i] = nn(att[...], w[:, cols_of(2 * turn(i) + c)]).astype(BF)
            return carry

        lax.fori_loop(0, NY, one, 0)

    def merge():
        for i in range(NY):
            sent[p_base + i].wait_recv()
            rbuf[i] = add(rbuf[i], precv[i])

    held = {"near": [], "yo": [], "seven": []}

    def beside(arrived, slot, part, into):
        arrived.wait_recv()
        held[into].append(send(gb.at[slot, part], gb.at[slot + (2 if slot < 6 else 1), part], sib))

    def ahead():
        for i in range(2):
            beside(first[i][0], 2, quarters[i], "near")
            beside(first[i][1], 3, quarters[i + 2], "near")

    def pass_on():
        for i in range(2):
            held["yo"].append((send(gb.at[2, quarters[i]], gb.at[6, quarters[i]], yp),
                               send(gb.at[3, quarters[i + 2]], gb.at[6, quarters[i + 2]], ym)))

    def near():
        for i in range(2):
            beside(later[i][0], 2, quarters[i + 2], "near")
            beside(later[i][1], 3, quarters[i], "near")

    def second():
        for copy in held["near"]:
            copy.wait_recv()
        terms(4, 6, second_group)

    def far():
        for i in range(2):
            beside(held["yo"][i][0], 6, quarters[i], "seven")
            beside(held["yo"][i][1], 6, quarters[i + 2], "seven")

    def third():
        for copy in held["seven"]:
            copy.wait_recv()
        terms(7, 8, third_group)

    def y_far():
        held["r_far"] = [send(rbuf.at[0, top], yrp.at[1, top], yp),
                         send(rbuf.at[0, bot], yrm.at[1, bot], ym)]

    def y_early():
        held["r"] = [send(rbuf.at[1, bot], yrp.at[0, bot], yp),
                     send(rbuf.at[3, top], yrm.at[0, top], ym)]

    def y_late():
        held["r_far"][0].wait_recv()
        rbuf[1, top] = add(rbuf[1, top], yrp[1, top])
        held["r"].append(send(rbuf.at[1, top], yrp.at[0, top], yp))
        held["r_far"][1].wait_recv()
        rbuf[3, bot] = add(rbuf[3, bot], yrm[1, bot])
        held["r"].append(send(rbuf.at[3, bot], yrm.at[0, bot], ym))

    def y_end():
        for copy in held["r"]:
            copy.wait_recv()
        mixed[...] = (rbuf[2].astype(F32) + yrp[0].astype(F32) + yrm[0].astype(F32)).astype(BF)
        out_mixed.start()

    def back():
        agw[...] = acc[...].astype(BF)
        tail = agw.at[pl.ds(5 * UNIT, UNIT)]
        held["back"] = [send(tail, back_recv.at[i], to) for i, to in enumerate((prv, nxt, acr))]

    def home():
        for copy in held["back"]:
            copy.wait_recv()
        got = from_prv | from_nxt | from_acr
        ghome[pl.ds(0, 5 * UNIT), :] = agw[pl.ds(0, 5 * UNIT), :]
        for u in (5, 6, 7):
            value = jnp.zeros((UNIT, INN), F32)
            for i, slot in enumerate((6, 7, 5)):
                hit = moved(dp, slot) & (starts[slot] == u * UNIT)
                value = jnp.where(hit, back_recv[i].astype(F32), value)
            if u == 5:
                value = jnp.where(got, value, unit(agw, 5))
            ghome[pl.ds(u * UNIT, UNIT), :] = value.astype(BF)

    def backward(h, carry):
        at = pl.multiple_of(h * HEAD, HEAD)
        q_t = qkv[0, :, pl.ds(at, HEAD)].astype(F32).T.astype(BF)
        g_t = ghome[:, pl.ds(at, HEAD)].astype(F32).T.astype(BF)
        dk_t[...] = jnp.zeros_like(dk_t)
        dv_t[...] = jnp.zeros_like(dv_t)
        for i, (lo, hi) in enumerate(WINDOWS):
            rows, keys = pl.ds(i * 128, 128), pl.ds(lo, hi - lo)
            k = qkv[1, keys, pl.ds(at, HEAD)]
            v = qkv[2, keys, pl.ds(at, HEAD)]
            p = probs[h, rows, keys]
            dp_ = nt(ghome[rows, pl.ds(at, HEAD)], v)
            mean = jnp.sum(p * dp_, axis=-1, keepdims=True)
            ds = (p * (dp_ - mean) * DOWN).astype(BF)
            dqkv[0, rows, pl.ds(at, HEAD)] = nn(ds, k).astype(BF)
            mine = slice(i * 128, (i + 1) * 128)
            dk_t[:, keys] += nn(q_t[:, mine], ds)
            dv_t[:, keys] += nn(g_t[:, mine], p.astype(BF))
        dqkv[1, :, pl.ds(at, HEAD)] = dk_t[...].T.astype(BF)
        dqkv[2, :, pl.ds(at, HEAD)] = dv_t[...].T.astype(BF)
        return carry

    def heads(lo, hi):
        lax.fori_loop(lo, hi, backward, 0)
        if hi == HEADS:
            out_dqkv.start()

    lanes = slice(None)
    x2a = along_x(2, 1, second_group)
    x2b = along_x(4, 1, second_group)
    x3 = along_x(6, 1, third_group)
    z2 = [along_z(wt2, i * ZROWS, ZROWS, z2p, z2m, zr2, lanes) for i in range(COLS // ZROWS)]
    z1 = [along_z(xr, i * XROWS, XROWS, z1p, z1m, wg, pl.ds(0, LX)) for i in range(PART // XROWS)]
    xl = [along_x_last()]

    def go(rings):
        for ring in rings:
            next(ring)

    todo = {
        "P": for_sibling, "Q": for_me, "M": merge, "S": ahead, "F": pass_on, "N": near, "T2A": lambda: terms(2, 4, second_group), "T2B": second, "W": far,
        "T3A": lambda: terms(6, 7, third_group), "T3B": third, "G2": lambda: grads(2, 6, second_group), "G3": lambda: grads(6, 8, third_group),
        "YF": y_far, "YE": y_early, "YL": y_late, "YD": y_end, "BK": back, "HM": home,
        "B0": lambda: heads(0, 1), "B1": lambda: heads(1, 2), "B2": lambda: heads(2, 3),
        "B12": lambda: heads(1, 3), "B": lambda: heads(0, 3),
        "X1": lambda: next(x1), "A": lambda: next(x2a), "C": lambda: next(x2b), "X3": lambda: next(x3),
        "Z2": lambda: go(z2), "Z1": lambda: go(z1), "XL": lambda: go(xl),
    }
    for name in ORDER:
        todo[name]()
    out_wg.start()
    for copy in sent:
        copy.wait_send()
    for copy in (out_mixed, out_dqkv, out_wg):
        copy.wait()


def scratch():
    v = pltpu.VMEM
    return [
        v((3, HOME, INN), BF), v((INN, 8 * COLS), BF), v((8, CAP, COLS), BF), v((HOME, HOME), F32),
        v((HEADS, HOME, HOME), F32), v((HOME, INN), BF), v((3, UNIT, INN), BF), v((3, UNIT, INN), BF),
        v((CAP, INN), BF), v((CAP, INN), F32), v((CAP, INN), BF), v((3, UNIT, INN), BF),
        v((HOME, INN), BF), v((HEAD, HOME), F32), v((HEAD, HOME), F32),
        v((8, COLS, LX), BF), v((8, COLS, LZ), BF),
        v((4, CAP, COLS), BF), v((4, CAP, COLS), BF), v((4, CAP, COLS), BF),
        v((2, CAP, COLS), BF), v((2, CAP, COLS), BF),
        v((4, PART, LX), BF), v((4, PART, LX), BF), v((8, PART, LX), BF), v((8, PART, LX), BF),
        v((8, PART, LX), BF),
        v((4, PART, LX), BF), v((4, PART, LX), BF), v((4, COLS, LZ), BF), v((4, COLS, LZ), BF),
        v((COLS, LZ), BF), v((2, PART, LZ), BF), v((2, PART, LZ), BF),
        v((CAP, COLS), BF), v((3, HOME, INN), BF), v((PART, INN), BF),
        pltpu.SemaphoreType.DMA((112,)), pltpu.SemaphoreType.DMA((112,)), pltpu.SemaphoreType.DMA((6,)),
    ]


def body(qkv_rows, out_weight, out_grad, image_len, dest_rank, dest_offset):
    smem = pl.BlockSpec(memory_space=pltpu.SMEM)
    anywhere = pl.BlockSpec(memory_space=pl.ANY)
    mixed, dqkv, turned = pl.pallas_call(
        kernel,
        out_shape=(
            jax.ShapeDtypeStruct((CAP, COLS), BF),
            jax.ShapeDtypeStruct((3, HOME, INN), BF),
            jax.ShapeDtypeStruct((192, INN), BF),
        ),
        in_specs=[smem, smem, anywhere, anywhere, anywhere],
        out_specs=(anywhere, anywhere, anywhere),
        scratch_shapes=scratch(),
        compiler_params=pltpu.CompilerParams(
            collective_id=0, has_side_effects=True, vmem_limit_bytes=60 * 2**20),
    )(image_len, dest_rank, jnp.transpose(qkv_rows, (1, 0, 2)), out_weight, out_grad)
    return mixed, jnp.transpose(dqkv, (1, 0, 2)), turned.T


def solution(mesh):
    return jax.shard_map(
        body,
        mesh=mesh,
        in_specs=(P("dp", None, "mp"), P("mp", None), P("dp", "mp"), P(), P(), P()),
        out_specs=(P("dp", "mp"), P("dp", None, "mp"), P("mp", "dp")),
        check_vma=False,
    )
```
